512 devices in a mesh: seq: 64 (over y, x, z_lo), ch: 8 (over z_hi, core).
Axes of the slice: x: 4, y: 8, z: 8 (z_hi: 4, z_lo: 2; z = z_hi * 2 + z_lo), core: 2. Of those that a mesh axis runs over, the one named last changes fastest.
Arguments:
- query_gate: bfloat16 [4096, 8192], P('ch', 'seq'), may hold values from -6 to 6
- key_gate: bfloat16 [4096, 8192], P('ch', 'seq'), may hold values from -6 to 6
- value_in: bfloat16 [4096, 8192], P('ch', 'seq'), may hold values from -6 to 6
- filter_weight: bfloat16 [512, 8192], P(None, 'seq'), may hold values from -6 to 6
- output_grad: bfloat16 [4096, 8192], P('ch', 'seq'), may hold values from -6 to 6
Outputs:
- query_grad: bfloat16 [4096, 8192], P('ch', 'seq')
- key_grad: bfloat16 [4096, 8192], P('ch', 'seq')
- value_grad: bfloat16 [4096, 8192], P('ch', 'seq')
- filter_grad: bfloat16 [512, 8192], P('ch', 'seq')
The draws below stay inside these ranges and needn't reach their ends.
All inputs are finite; a program needn't handle non-finite values.
Results may differ from the reference program's by a relative error of at most 0.0057.
Values may be sent and summed in bfloat16 or wider, within the bound.
A program may use at most 64 MiB of HBM per device.

```python
import jax
import jax.numpy as jnp
from jax import lax

CH = 4096
FILTERS = 512
LENGTH = 8192


def block_scale(stream_key, shape, cuts, smallest, largest):
    level, own = 1.0, jax.random.fold_in(stream_key, 6)
    for dim, blocks in cuts:
        steps = jnp.exp(jax.random.uniform(jax.random.fold_in(own, dim), (blocks,), jnp.float32, smallest / len(cuts), largest / len(cuts)))
        level = level * jnp.repeat(steps, shape[dim] // blocks).reshape([-1 if axis == dim else 1 for axis in range(len(shape))])
    return level


def centred(key, extent, spread, most, split=(), dtype=jnp.bfloat16):
    values = jax.random.normal(key, extent, jnp.float32) * spread
    if len(split) > 0:
        values = block_scale(key, extent, split, -0.22, 0.18) * values
    return jnp.clip(values, min=-most, max=most).astype(dtype)


def setup_inputs(seed: int = 0) -> dict:
    streams_of = jax.random.split(jax.random.key(seed), 6)
    query_gate = centred(streams_of[0], (CH, LENGTH), 1.0, 6.0, ((0, 8), (1, 64)))
    key_gate = centred(streams_of[1], (CH, LENGTH), 1.0, 6.0, ((0, 8), (1, 64)))
    value_in = centred(streams_of[2], (CH, LENGTH), 1.0, 6.0, ((0, 8), (1, 64)))
    filter_weight = centred(streams_of[3], (FILTERS, LENGTH), 1.0, 6.0, ((1, 64),))
    output_grad = centred(streams_of[4], (CH, LENGTH), 1.0, 6.0, ((0, 8), (1, 64)))
    return dict(query_gate=query_gate, key_gate=key_gate, value_in=value_in, filter_weight=filter_weight, output_grad=output_grad)


def reference(query_gate, key_gate, value_in, filter_weight, output_grad):
    size_full = 2 * LENGTH
    norm_factor = LENGTH ** -0.5
    group_count = CH // FILTERS
    spec_filter = jnp.fft.rfft(filter_weight.astype(jnp.float32), n=size_full, axis=1) * norm_factor

    def per_group(carry, pieces):
        query_part, key_part, value_part, grad_part = pieces
        gated_in = (key_part.astype(jnp.float32) * value_part.astype(jnp.float32)).astype(jnp.bfloat16)
        inner_grad = (grad_part.astype(jnp.float32) * query_part.astype(jnp.float32)).astype(jnp.bfloat16)
        spec_in = jnp.fft.rfft(gated_in.astype(jnp.float32), n=size_full, axis=1)
        spec_grad = jnp.fft.rfft(inner_grad.astype(jnp.float32), n=size_full, axis=1)
        conv_out = jnp.fft.irfft(spec_filter * spec_in, n=size_full, axis=1)[:, :LENGTH].astype(jnp.bfloat16)
        in_grad = jnp.fft.irfft(jnp.conj(spec_filter) * spec_grad, n=size_full, axis=1)[:, :LENGTH].astype(jnp.bfloat16)
        query_grad = (grad_part.astype(jnp.float32) * conv_out.astype(jnp.float32)).astype(jnp.bfloat16)
        key_grad = (in_grad.astype(jnp.float32) * value_part.astype(jnp.float32)).astype(jnp.bfloat16)
        value_grad = (in_grad.astype(jnp.float32) * key_part.astype(jnp.float32)).astype(jnp.bfloat16)
        carry = carry + spec_grad * jnp.conj(spec_in)
        return carry, (query_grad, key_grad, value_grad)

    def split_groups(array):
        return array.reshape(group_count, FILTERS, LENGTH)

    start_cross = jnp.zeros_like(spec_filter)
    cross_sum, grads = lax.scan(per_group, start_cross, (split_groups(query_gate), split_groups(key_gate), split_groups(value_in), split_groups(output_grad)))
    filter_grad = (jnp.fft.irfft(cross_sum, n=size_full, axis=1)[:, :LENGTH] * norm_factor).astype(jnp.bfloat16)
    query_grad = grads[0].reshape(CH, LENGTH)
    key_grad = grads[1].reshape(CH, LENGTH)
    value_grad = grads[2].reshape(CH, LENGTH)
    return (query_grad, key_grad, value_grad, filter_grad)
```

```python
import functools
import math

import jax
import jax.numpy as jnp
from jax import lax
from jax.experimental import pallas as pl
from jax.experimental.pallas import tpu as pltpu
from jax.sharding import PartitionSpec as P

TB = 128
BLK = 256
PARTS = 4
ORDER = (2, 1, 3, 0)
BF16 = jnp.bfloat16
F32 = jnp.float32


def dot(left, right, contract=((1,), (0,))):
    return lax.dot_general(left, right, (contract, ((), ())), preferred_element_type=F32)


def reversal(size):
    rows = lax.broadcasted_iota(jnp.int32, (size, size), 0)
    cols = lax.broadcasted_iota(jnp.int32, (size, size), 1)
    return (rows + cols == size - 1).astype(F32).astype(BF16)


def kernel(
    ns, nc,
    q_hbm, k_hbm, v_hbm, w_hbm, og_hbm,
    qg_out, kg_out, vg_out, fg_out,
    q_v, k_v, v_v, w_v, og_v,
    xa, ra, sd, mb, rb, fs, rf,
    ht, xf, xz0, xz8, gb, gjf, glt, lhs, acc, yst,
    xd, rd, mc, rc, fgm, fgs, rfg, rcf,
    in_sem, a_send, a_recv, b_send, b_recv, f_send, f_recv,
    d_send, d_recv, c_send, c_recv, g_send, g_recv,
):
    me_s, me_c = lax.axis_index("seq"), lax.axis_index("ch")
    pr = ns // PARTS
    nb = ns * TB // BLK
    rows = nb * nc
    msg = 2 * nc
    norm = float((ns * TB) ** -0.5)
    my_part = me_s // pr

    def copy_in(i, src, dst):
        return pltpu.make_async_copy(src, dst, in_sem.at[i])

    loads = [
        copy_in(0, k_hbm, k_v),
        copy_in(1, v_hbm, v_v),
        copy_in(2, og_hbm, og_v),
        copy_in(3, q_hbm, q_v),
        copy_in(4, w_hbm.at[pl.ds(pl.multiple_of(me_c * ns, ns), ns)], w_v),
    ]
    for load in loads:
        load.start()

    barrier = pltpu.get_barrier_semaphore()

    def greet_seq(o, carry):
        pl.semaphore_signal(barrier, inc=1, device_id={"seq": lax.rem(me_s + o, ns)})
        return carry

    def greet_ch(o, carry):
        pl.semaphore_signal(barrier, inc=1, device_id={"ch": lax.rem(me_c + o, nc)})
        return carry

    lax.fori_loop(1, nc, greet_ch, 0)
    lax.fori_loop(1, ns, greet_seq, 0)

    for load in loads:
        load.wait()

    def products(c, carry):
        for m in range(PARTS):
            at = pl.ds(pl.multiple_of(c * ns + m * pr, pr), pr)
            xa[m, c, 0] = (k_v[at].astype(F32) * v_v[at].astype(F32)).astype(BF16)
            xa[m, c, 1] = (og_v[at].astype(F32) * q_v[at].astype(F32)).astype(BF16)
        return carry

    lax.fori_loop(0, nc, products, 0)
    wf = w_v[...].astype(F32)
    for s in range(ns):
        fs[s] = wf[s : s + 1]

    pl.semaphore_wait(barrier, ns - 1 + nc - 1)

    def start_ch(out_ref, in_ref, send_sem, recv_sem):
        for kappa in ORDER:
            m = lax.rem(my_part + kappa, PARTS)

            def push(o, carry):
                c = lax.rem(me_c + o, nc)
                pltpu.make_async_remote_copy(
                    out_ref.at[m, c], in_ref.at[m, me_c], send_sem, recv_sem.at[kappa],
                    device_id={"ch": c},
                ).start()
                return carry

            lax.fori_loop(1, nc, push, 0)
            pltpu.make_async_copy(out_ref.at[m, me_c], in_ref.at[m, me_c], recv_sem.at[kappa]).start()

    def turn_part(kappa, in_ref, mid_ref, recv_sem):
        m = lax.rem(my_part + kappa, PARTS)
        pltpu.make_async_copy(in_ref.at[m], in_ref.at[m], recv_sem.at[kappa]).wait()
        sd[...] = in_ref[m].astype(F32).reshape(nc * 2 * pr, TB)
        for i in range(pr):
            upper = sd[pl.ds(i, nc, stride=2 * pr), :]
            lower = sd[pl.ds(pr + i, nc, stride=2 * pr), :]
            mid_ref[kappa, i] = jnp.concatenate([upper, lower], axis=0).astype(BF16)

    def start_seq_part(kappa, mid_ref, end_ref, send_sem, recv_sem):
        m = lax.rem(my_part + kappa, PARTS)
        mine = lax.rem(me_s, pr)

        def push(o, carry):
            i = lax.rem(mine + o, pr)
            pltpu.make_async_remote_copy(
                mid_ref.at[kappa, i], end_ref.at[me_s], send_sem, recv_sem,
                device_id={"seq": m * pr + i},
            ).start()
            return carry

        lax.fori_loop(1 if kappa == 0 else 0, pr, push, 0)
        if kappa == 0:
            pltpu.make_async_copy(mid_ref.at[kappa, mine], end_ref.at[me_s], recv_sem).start()

    def start_rows(out_ref, in_ref, send_sem, recv_sem):
        def push(o, carry):
            s = lax.rem(me_s + o, ns)
            pltpu.make_async_remote_copy(
                out_ref.at[s], in_ref.at[me_s], send_sem, recv_sem, device_id={"seq": s}
            ).start()
            return carry

        lax.fori_loop(1, ns, push, 0)
        pltpu.make_async_copy(out_ref.at[me_s], in_ref.at[me_s], recv_sem).start()

    def wait_all(ref, sem):
        pltpu.make_async_copy(ref, ref, sem).wait()

    start_ch(xa, ra, a_send, a_recv)
    start_rows(fs, rf, f_send, f_recv)
    for kappa in ORDER:
        turn_part(kappa, ra, mb, a_recv)
        start_seq_part(kappa, mb, rb, b_send, b_recv)

    wait_all(rf, f_recv)
    sub = lax.broadcasted_iota(jnp.int32, (TB, TB), 0)
    lane = lax.broadcasted_iota(jnp.int32, (TB, TB), 1)
    keep = lane >= sub
    ht[:, 0:TB] = jnp.zeros((TB, TB), BF16)

    def toeplitz(e, before):
        turned = pltpu.roll(jnp.broadcast_to(rf[e], (TB, TB)), 0, 1, stride=1, stride_axis=0)
        at = pl.ds(pl.multiple_of((e + 1) * TB, TB), TB)
        ht[:, at] = jnp.where(keep, turned, before).astype(BF16)
        return turned

    lax.fori_loop(0, ns, toeplitz, jnp.zeros((TB, TB), F32))
    acc[...] = jnp.zeros_like(acc)
    xf[0:rows] = jnp.zeros((rows, BLK), F32)
    xf[2 * rows :] = jnp.zeros((nc, BLK), F32)
    flip = reversal(BLK)

    wait_all(rb, b_recv)

    def gather(j, carry):
        low, high = rb[2 * j].astype(F32), rb[2 * j + 1].astype(F32)
        at = pl.ds(pl.multiple_of(rows + j * nc, nc), nc)
        xf[at, 0:TB] = low[0:nc]
        xf[at, TB:BLK] = high[0:nc]
        at = pl.ds(pl.multiple_of(j * nc, nc), nc)
        gjf[at, 0:TB] = low[nc:msg]
        gjf[at, TB:BLK] = high[nc:msg]
        return carry

    lax.fori_loop(0, nb, gather, 0)
    gb[...] = gjf[...].astype(BF16)
    gjf[...] = dot(gb[...], flip)

    def interleave(j, carry):
        x_at = pl.ds(pl.multiple_of(rows + j * nc, nc), nc)
        g_at = pl.ds(pl.multiple_of((nb - 1 - j) * nc, nc), nc)
        both = jnp.concatenate([xf[x_at], gjf[g_at]], axis=0)
        lhs[pl.ds(pl.multiple_of(j * msg, msg), msg)] = both.astype(BF16)
        return carry

    lax.fori_loop(0, nb, interleave, 0)

    group = nb // PARTS
    for grp in range(PARTS):
        count = (nb - grp * group) * msg

        def lag(i, carry):
            d = grp * group + i
            low = pl.multiple_of(d * BLK, BLK)
            block = jnp.concatenate([ht[:, pl.ds(low + TB, BLK)], ht[:, pl.ds(low, BLK)]], axis=0)
            at = pl.ds(pl.multiple_of(d * msg, msg), count)
            acc[at] += dot(lhs[0:count], block)
            return carry

        lax.fori_loop(0, group, lag, 0)

    def scatter_x(j, carry):
        out = acc[pl.ds(pl.multiple_of(j * msg, msg), nc)] * norm
        yst[pl.ds(pl.multiple_of(2 * j * msg, msg), nc)] = out[:, 0:TB]
        yst[pl.ds(pl.multiple_of((2 * j + 1) * msg, msg), nc)] = out[:, TB:BLK]
        gjf[pl.ds(pl.multiple_of((nb - 1 - j) * nc, nc), nc)] = (
            acc[pl.ds(pl.multiple_of(j * msg + nc, nc), nc)] * norm
        )
        return carry

    lax.fori_loop(0, nb, scatter_x, 0)
    gjf[...] = dot(gjf[...].astype(BF16), flip)

    def scatter_g(j, carry):
        out = gjf[pl.ds(pl.multiple_of(j * nc, nc), nc)]
        yst[pl.ds(pl.multiple_of(2 * j * msg + nc, nc), nc)] = out[:, 0:TB]
        yst[pl.ds(pl.multiple_of((2 * j + 1) * msg + nc, nc), nc)] = out[:, TB:BLK]
        return carry

    lax.fori_loop(0, nb, scatter_g, 0)

    for m in range(PARTS):
        for c in range(nc):
            for part in range(2):
                first = m * pr * msg + part * nc + c
                xd[m, c, part] = yst[pl.ds(first, pr, stride=msg), :].astype(BF16)
    start_ch(xd, rd, d_send, d_recv)

    glt[...] = dot(flip, gb[...], ((1,), (1,))).astype(BF16)
    xz0[...] = xf[0 : 2 * rows].astype(BF16)
    xz8[...] = xf[nc : 2 * rows + nc].astype(BF16)

    def diagonals(tile, before, at):
        turned = pltpu.roll(tile, 0, 1, stride=1, stride_axis=0)
        fgm[pl.ds(at, 1)] = jnp.sum(jnp.where(keep, turned, before), axis=0, keepdims=True)
        return turned

    def two_lags(i, carry):
        over, before = carry
        odd = pl.multiple_of((2 * i) * nc, msg)
        even = pl.multiple_of((2 * i + 2) * nc, msg)
        for half, shifted in ((0, xz8[pl.ds(odd, rows)]), (1, xz0[pl.ds(even, rows)])):
            prod = dot(glt[...], shifted)
            at = 4 * i + 2 * half
            before = diagonals(prod[0:TB, 0:TB] + over, before, at)
            before = diagonals(prod[0:TB, TB:BLK] + prod[TB:BLK, 0:TB], before, at + 1)
            over = prod[TB:BLK, TB:BLK]
        return over, before

    zero = jnp.zeros((TB, TB), F32)
    lax.fori_loop(0, nb // 2, two_lags, (zero, zero))

    for kappa in ORDER:
        turn_part(kappa, rd, mc, d_recv)
        start_seq_part(kappa, mc, rc, c_send, c_recv)

    fgm[...] = dot((fgm[...] * norm).astype(BF16), reversal(TB))
    for s in range(ns):
        fgs[s] = fgm[ns - 1 - s : ns - s]
    start_rows(fgs, rfg, g_send, g_recv)

    wait_all(rc, c_recv)
    rcf[...] = rc[...].astype(F32).reshape(ns * msg, TB)
    for c in range(nc):
        at = pl.ds(c * ns, ns)
        conv = rcf[pl.ds(c, ns, stride=msg), :]
        grad = rcf[pl.ds(nc + c, ns, stride=msg), :]
        qg_out[at] = (og_v[at].astype(F32) * conv).astype(BF16)
        kg_out[at] = (grad * v_v[at].astype(F32)).astype(BF16)
        vg_out[at] = (grad * k_v[at].astype(F32)).astype(BF16)

    wait_all(rfg, g_recv)
    for s in range(ns):
        fgm[s : s + 1] = rfg[s]
    fg_out[...] = fgm[...].astype(BF16)

    wait_all(xa.at[:, pl.ds(0, nc - 1)], a_send)
    wait_all(xd.at[:, pl.ds(0, nc - 1)], d_send)
    for ref, sem in ((rb, b_send), (rc, c_send), (fs, f_send), (fgs, g_send)):
        wait_all(ref.at[pl.ds(0, ns - 1)], sem)


def shards(ns, nc, query_gate, key_gate, value_in, filter_weight, output_grad):
    local = query_gate.shape[0]
    nb = ns * TB // BLK
    rows, msg, pr = nb * nc, 2 * nc, ns // PARTS
    bf, f32 = (lambda *shape: pltpu.VMEM(shape, BF16)), (lambda *shape: pltpu.VMEM(shape, F32))
    one = pltpu.SemaphoreType.DMA(())
    some = pltpu.SemaphoreType.DMA((PARTS,))
    any_spec = pl.BlockSpec(memory_space=pl.ANY)
    vmem_spec = pl.BlockSpec(memory_space=pltpu.VMEM)
    wide = jax.ShapeDtypeStruct((local, TB), BF16)
    return pl.pallas_call(
        functools.partial(kernel, ns, nc),
        out_shape=(wide, wide, wide, jax.ShapeDtypeStruct((ns, TB), BF16)),
        in_specs=[any_spec] * 5,
        out_specs=(vmem_spec,) * 4,
        scratch_shapes=[
            bf(local, TB), bf(local, TB), bf(local, TB), bf(ns, TB), bf(local, TB),
            bf(PARTS, nc, 2, pr, TB), bf(PARTS, nc, 2, pr, TB), f32(nc * 2 * pr, TB),
            bf(PARTS, pr, msg, TB), bf(ns, msg, TB), f32(ns, 1, TB), f32(ns, 1, TB),
            bf(TB, (ns + 1) * TB), f32(2 * rows + nc, BLK), bf(2 * rows, BLK), bf(2 * rows, BLK),
            bf(rows, BLK), f32(rows, BLK), bf(BLK, rows), bf(2 * rows, BLK),
            f32(2 * rows + 2 * rows // PARTS, BLK), f32(ns * msg, TB),
            bf(PARTS, nc, 2, pr, TB), bf(PARTS, nc, 2, pr, TB),
            bf(PARTS, pr, msg, TB), bf(ns, msg, TB), f32(ns, TB), f32(ns, 1, TB), f32(ns, 1, TB),
            f32(ns * msg, TB),
            pltpu.SemaphoreType.DMA((5,)), one, some, one, one, one, one,
            one, some, one, one, one, one,
        ],
        compiler_params=pltpu.CompilerParams(
            collective_id=0, has_side_effects=True, vmem_limit_bytes=40 * 1024 * 1024
        ),
    )(query_gate, key_gate, value_in, filter_weight, output_grad)


def solution(mesh):
    ns, nc = mesh.shape["seq"], mesh.shape["ch"]
    placed = (P("ch", "seq"), P("ch", "seq"), P("ch", "seq"), P(None, "seq"), P("ch", "seq"))
    return jax.shard_map(
        functools.partial(shards, ns, nc),
        mesh=mesh,
        in_specs=placed,
        out_specs=(P("ch", "seq"),) * 4,
        check_vma=False,
    )
```

```python
import functools
import math

import jax
import jax.numpy as jnp
from jax import lax
from jax.experimental import pallas as pl
from jax.experimental.pallas import tpu as pltpu
from jax.sharding import PartitionSpec as P

TB = 128
BLK = 256
PARTS = 4
ORDER = (2, 1, 3, 0)
LAGS = 4
VMEM_BYTES = 60 * 1024 * 1024
BF16 = jnp.bfloat16
F32 = jnp.float32


def dot(left, right, contract=((1,), (0,))):
    return lax.dot_general(left, right, (contract, ((), ())), preferred_element_type=F32)


def reversal(size):
    rows = lax.broadcasted_iota(jnp.int32, (size, size), 0)
    cols = lax.broadcasted_iota(jnp.int32, (size, size), 1)
    return (rows + cols == size - 1).astype(F32).astype(BF16)


def kernel(
    ns, nc, nu,
    q_hbm, k_hbm, v_hbm, w_hbm, og_hbm,
    rc, g2,
    q_v, k_v, v_v, w_v, og_v,
    xa, ra, sd, mb, rb, fs, f1, f1s, f2,
    tt, xf, xz0, xz8, gb, gjf, glt, lhs, acc, yst,
    xd, rd, mc, fgm, g1, g1s,
    in_sem, a_send, a_recv, b_send, b_recv, f_send, f_recv,
    d_send, d_recv, c_send, c_recv, g_send, g_recv,
):
    me_s, me_c = lax.axis_index("seq"), lax.axis_index("ch")
    ny = ns // nu
    me_y, me_u = me_s // nu, lax.rem(me_s, nu)
    pr = ns // PARTS
    nb = ns * TB // BLK
    rows = nb * nc
    msg = 2 * nc
    norm = float((ns * TB) ** -0.5)
    my_part = me_s // pr

    def copy_in(i, src, dst):
        return pltpu.make_async_copy(src, dst, in_sem.at[i])

    loads = [
        copy_in(0, k_hbm, k_v),
        copy_in(1, v_hbm, v_v),
        copy_in(2, og_hbm, og_v),
        copy_in(3, q_hbm, q_v),
        copy_in(4, w_hbm.at[pl.ds(pl.multiple_of(me_c * ns, ns), ns)], w_v),
    ]
    for load in loads:
        load.start()

    barrier = pltpu.get_barrier_semaphore()

    def greet_seq(o, carry):
        pl.semaphore_signal(barrier, inc=1, device_id={"seq": lax.rem(me_s + o, ns)})
        return carry

    def greet_ch(o, carry):
        pl.semaphore_signal(barrier, inc=1, device_id={"ch": lax.rem(me_c + o, nc)})
        return carry

    lax.fori_loop(1, nc, greet_ch, 0)
    lax.fori_loop(1, ns, greet_seq, 0)

    for load in loads:
        load.wait()

    for c in range(nc):
        for m in range(PARTS):
            at = pl.ds(c * ns + m * pr, pr)
            xa[m, c, 0] = (k_v[at].astype(F32) * v_v[at].astype(F32)).astype(BF16)
            xa[m, c, 1] = (og_v[at].astype(F32) * q_v[at].astype(F32)).astype(BF16)
    fs[...] = w_v[...].astype(F32)

    pl.semaphore_wait(barrier, ns - 1 + nc - 1)

    def tile(ref, i, size):
        return ref.at[pl.ds(pl.multiple_of(i * size, size), size)]

    def start_y(out_ref, in_ref, send_sem, recv_sem):
        def push(o, carry):
            y = lax.rem(me_y + o, ny)
            pltpu.make_async_remote_copy(
                tile(out_ref, y, nu), tile(in_ref, me_y, nu), send_sem.at[0], recv_sem.at[0],
                device_id={"seq": y * nu + me_u},
            ).start()
            return carry

        lax.fori_loop(1, ny, push, 0)
        pltpu.make_async_copy(
            tile(out_ref, me_y, nu), tile(in_ref, me_y, nu), recv_sem.at[0]
        ).start()

    def turn_y_start_u(in_ref, mid_ref, end_ref, send_sem, recv_sem):
        wait_all(in_ref, recv_sem.at[0])
        for u in range(nu):
            mid_ref[u * ny : (u + 1) * ny] = in_ref[pl.ds(u, ny, stride=nu), :]

        def push(o, carry):
            u = lax.rem(me_u + o, nu)
            pltpu.make_async_remote_copy(
                tile(mid_ref, u, ny), tile(end_ref, me_u, ny), send_sem.at[1], recv_sem.at[1],
                device_id={"seq": me_y * nu + u},
            ).start()
            return carry

        lax.fori_loop(1, nu, push, 0)
        pltpu.make_async_copy(
            tile(mid_ref, me_u, ny), tile(end_ref, me_u, ny), recv_sem.at[1]
        ).start()

    def start_ch(out_ref, in_ref, send_sem, recv_sem):
        for kappa in ORDER:
            m = lax.rem(my_part + kappa, PARTS)

            def push(o, carry):
                c = lax.rem(me_c + o, nc)
                pltpu.make_async_remote_copy(
                    out_ref.at[m, c], in_ref.at[m, me_c], send_sem, recv_sem.at[kappa],
                    device_id={"ch": c},
                ).start()
                return carry

            lax.fori_loop(1, nc, push, 0)
            pltpu.make_async_copy(out_ref.at[m, me_c], in_ref.at[m, me_c], recv_sem.at[kappa]).start()

    def turn_part(kappa, in_ref, mid_ref, recv_sem):
        m = lax.rem(my_part + kappa, PARTS)
        wait_all(in_ref.at[m], recv_sem.at[kappa])
        sd[...] = in_ref[m].astype(F32).reshape(nc * 2 * pr, TB)
        for i in range(pr):
            upper = sd[pl.ds(i, nc, stride=2 * pr), :]
            lower = sd[pl.ds(pr + i, nc, stride=2 * pr), :]
            mid_ref[kappa, i] = jnp.concatenate([upper, lower], axis=0).astype(BF16)

    def start_seq_part(kappa, mid_ref, end_ref, send_sem, recv_sem):
        m = lax.rem(my_part + kappa, PARTS)
        mine = lax.rem(me_s, pr)

        def push(o, carry):
            i = lax.rem(mine + o, pr)
            pltpu.make_async_remote_copy(
                mid_ref.at[kappa, i], end_ref.at[me_s], send_sem, recv_sem,
                device_id={"seq": m * pr + i},
            ).start()
            return carry

        lax.fori_loop(1 if kappa == 0 else 0, pr, push, 0)
        if kappa == 0:
            pltpu.make_async_copy(mid_ref.at[kappa, mine], end_ref.at[me_s], recv_sem).start()

    def wait_all(ref, sem):
        pltpu.make_async_copy(ref, ref, sem).wait()

    start_y(fs, f1, f_send, f_recv)
    start_ch(xa, ra, a_send, a_recv)
    turn_y_start_u(f1, f1s, f2, f_send, f_recv)
    for kappa in ORDER:
        turn_part(kappa, ra, mb, a_recv)
        start_seq_part(kappa, mb, rb, b_send, b_recv)

    sub = lax.broadcasted_iota(jnp.int32, (TB, TB), 0)
    lane = lax.broadcasted_iota(jnp.int32, (TB, TB), 1)
    keep = lane >= sub
    zero = jnp.zeros((TB, TB), F32)
    flip = reversal(BLK)
    wait_all(f2, f_recv.at[1])

    def skewed(tile):
        return pltpu.roll(tile, 0, 1, stride=1, stride_axis=0)

    def filter_row(s):
        return jnp.broadcast_to(f2[pl.ds(s % nu * ny + s // nu, 1), :], (TB, TB))

    tt[TB:BLK, 0:TB] = zero.astype(BF16)
    before = zero
    for d in range(nb):
        even, odd = skewed(filter_row(2 * d)), skewed(filter_row(2 * d + 1))
        block = jnp.where(keep, even, before).astype(BF16)
        tt[d * BLK : d * BLK + TB, 0:TB] = block
        tt[d * BLK + TB : (d + 1) * BLK, TB:BLK] = block
        block = jnp.where(keep, odd, even).astype(BF16)
        tt[d * BLK : d * BLK + TB, TB:BLK] = block
        tt[(d + 1) * BLK + TB : (d + 2) * BLK, 0:TB] = block
        before = odd

    lhs[0 : LAGS * msg] = jnp.zeros((LAGS * msg, BLK), BF16)
    xf[0:rows] = jnp.zeros((rows, BLK), F32)
    xf[2 * rows :] = jnp.zeros((nc, BLK), F32)

    wait_all(rb, b_recv)
    for j in range(nb):
        low, high = rb[2 * j].astype(F32), rb[2 * j + 1].astype(F32)
        xf[rows + j * nc : rows + (j + 1) * nc, 0:TB] = low[0:nc]
        xf[rows + j * nc : rows + (j + 1) * nc, TB:BLK] = high[0:nc]
        gjf[j * nc : (j + 1) * nc, 0:TB] = low[nc:msg]
        gjf[j * nc : (j + 1) * nc, TB:BLK] = high[nc:msg]
    gb[...] = gjf[...].astype(BF16)
    gjf[...] = dot(gb[...], flip)
    for j in range(nb):
        back = nb - 1 - j
        both = jnp.concatenate(
            [xf[rows + j * nc : rows + (j + 1) * nc], gjf[back * nc : (back + 1) * nc]], axis=0
        )
        lhs[(LAGS + j) * msg : (LAGS + j + 1) * msg] = both.astype(BF16)

    for first in range(0, nb, LAGS):
        count = (nb - first) * msg
        left = jnp.concatenate(
            [lhs[(LAGS - e) * msg : (LAGS - e) * msg + count] for e in range(LAGS)], axis=1
        )
        prod = dot(left, tt[first * BLK : (first + LAGS) * BLK])
        if first == 0:
            acc[...] = prod
        else:
            acc[first * msg :] += prod

    for j in range(nb):
        back = nb - 1 - j
        out = acc[j * msg : j * msg + nc] * norm
        yst[2 * j * msg : 2 * j * msg + nc] = out[:, 0:TB]
        yst[(2 * j + 1) * msg : (2 * j + 1) * msg + nc] = out[:, TB:BLK]
        gjf[back * nc : (back + 1) * nc] = acc[j * msg + nc : (j + 1) * msg] * norm
    gjf[...] = dot(gjf[...].astype(BF16), flip)
    for j in range(nb):
        out = gjf[j * nc : (j + 1) * nc]
        yst[2 * j * msg + nc : (2 * j + 1) * msg] = out[:, 0:TB]
        yst[(2 * j + 1) * msg + nc : (2 * j + 2) * msg] = out[:, TB:BLK]

    for m in range(PARTS):
        for c in range(nc):
            for part in range(2):
                begin = m * pr * msg + part * nc + c
                xd[m, c, part] = yst[pl.ds(begin, pr, stride=msg), :].astype(BF16)
    start_ch(xd, rd, d_send, d_recv)

    glt[...] = dot(flip, gb[...], ((1,), (1,))).astype(BF16)
    xz0[...] = xf[0 : 2 * rows].astype(BF16)
    xz8[...] = xf[nc : 2 * rows + nc].astype(BF16)
    over, before = zero, zero
    for i in range(nb):
        low = (i // 2) * msg
        shifted = xz0[low + msg : low + msg + rows] if i % 2 else xz8[low : low + rows]
        prod = dot(glt[...], shifted)
        pair = (prod[0:TB, 0:TB] + over, prod[0:TB, TB:BLK] + prod[TB:BLK, 0:TB])
        for half, total in enumerate(pair):
            at = ns - 1 - (2 * i + half)
            turned = skewed(total)
            fgm[at : at + 1] = jnp.sum(jnp.where(keep, turned, before), axis=0, keepdims=True)
            before = turned
        over = prod[TB:BLK, TB:BLK]
    fgm[...] = dot((fgm[...] * norm).astype(BF16), reversal(TB))
    start_y(fgm, g1, g_send, g_recv)

    for kappa in ORDER:
        turn_part(kappa, rd, mc, d_recv)
        start_seq_part(kappa, mc, rc, c_send, c_recv)
    turn_y_start_u(g1, g1s, g2, g_send, g_recv)

    wait_all(rc, c_recv)
    wait_all(g2, g_recv.at[1])
    wait_all(xa.at[:, pl.ds(0, nc - 1)], a_send)
    wait_all(xd.at[:, pl.ds(0, nc - 1)], d_send)
    for ref, sem in ((rb, b_send), (rc, c_send)):
        wait_all(ref.at[pl.ds(0, ns - 1)], sem)
    for sem in (f_send, g_send):
        wait_all(f1.at[pl.ds(0, ns - nu)], sem.at[0])
        wait_all(f2.at[pl.ds(0, ns - ny)], sem.at[1])


def finish(ns, nc, nu, rc, g2, k_v, v_v, og_v, qg_out, kg_out, vg_out, fg_out, rcf):
    msg, ny = 2 * nc, ns // nu
    rcf[...] = rc[...].astype(F32).reshape(ns * msg, TB)
    for c in range(nc):
        at = pl.ds(c * ns, ns)
        conv = rcf[pl.ds(c, ns, stride=msg), :]
        grad = rcf[pl.ds(nc + c, ns, stride=msg), :]
        qg_out[at] = (og_v[at].astype(F32) * conv).astype(BF16)
        kg_out[at] = (grad * v_v[at].astype(F32)).astype(BF16)
        vg_out[at] = (grad * k_v[at].astype(F32)).astype(BF16)
    for y in range(0, ny, 2):
        two = [g2[pl.ds(y + i, nu, stride=ny), :] for i in range(2)]
        fg_out[y * nu : (y + 2) * nu] = jnp.concatenate(two, axis=0).astype(BF16)


def shards(ns, nc, query_gate, key_gate, value_in, filter_weight, output_grad):
    local = query_gate.shape[0]
    nb, nu = ns * TB // BLK, math.isqrt(ns)
    ny = ns // nu
    rows, msg, pr = nb * nc, 2 * nc, ns // PARTS
    bf, f32 = (lambda *shape: pltpu.VMEM(shape, BF16)), (lambda *shape: pltpu.VMEM(shape, F32))
    one = pltpu.SemaphoreType.DMA(())
    two = pltpu.SemaphoreType.DMA((2,))
    some = pltpu.SemaphoreType.DMA((PARTS,))
    any_spec = pl.BlockSpec(memory_space=pl.ANY)
    vmem_spec = pl.BlockSpec(memory_space=pltpu.VMEM)
    moved, filter_part = pl.pallas_call(
        functools.partial(kernel, ns, nc, nu),
        out_shape=(
            jax.ShapeDtypeStruct((ns, msg, TB), BF16),
            jax.ShapeDtypeStruct((ns, TB), F32),
        ),
        in_specs=[any_spec] * 5,
        out_specs=(any_spec,) * 2,
        scratch_shapes=[
            bf(local, TB), bf(local, TB), bf(local, TB), bf(ns, TB), bf(local, TB),
            bf(PARTS, nc, 2, pr, TB), bf(PARTS, nc, 2, pr, TB), f32(nc * 2 * pr, TB),
            bf(PARTS, pr, msg, TB), bf(ns, msg, TB),
            f32(ns, TB), f32(ns, TB), f32(ns, TB), f32(ns, TB),
            bf((nb + 1) * BLK, BLK), f32(2 * rows + nc, BLK), bf(2 * rows, BLK), bf(2 * rows, BLK),
            bf(rows, BLK), f32(rows, BLK), bf(BLK, rows), bf((LAGS + nb) * msg, BLK),
            f32(nb * msg, BLK), f32(ns * msg, TB),
            bf(PARTS, nc, 2, pr, TB), bf(PARTS, nc, 2, pr, TB),
            bf(PARTS, pr, msg, TB), f32(ns, TB), f32(ns, TB), f32(ns, TB),
            pltpu.SemaphoreType.DMA((5,)), one, some, one, one, two, two,
            one, some, one, one, two, two,
        ],
        compiler_params=pltpu.CompilerParams(
            collective_id=0, has_side_effects=True, vmem_limit_bytes=VMEM_BYTES
        ),
    )(query_gate, key_gate, value_in, filter_weight, output_grad)
    wide = jax.ShapeDtypeStruct((local, TB), BF16)
    return pl.pallas_call(
        functools.partial(finish, ns, nc, nu),
        out_shape=(wide, wide, wide, jax.ShapeDtypeStruct((ns, TB), BF16)),
        in_specs=[vmem_spec] * 5,
        out_specs=(vmem_spec,) * 4,
        scratch_shapes=[f32(ns * msg, TB)],
        compiler_params=pltpu.CompilerParams(vmem_limit_bytes=VMEM_BYTES),
    )(moved, filter_part, key_gate, value_in, output_grad)


def solution(mesh):
    ns, nc = mesh.shape["seq"], mesh.shape["ch"]
    placed = (P("ch", "seq"), P("ch", "seq"), P("ch", "seq"), P(None, "seq"), P("ch", "seq"))
    return jax.shard_map(
        functools.partial(shards, ns, nc),
        mesh=mesh,
        in_specs=placed,
        out_specs=(P("ch", "seq"),) * 4,
        check_vma=False,
    )
```

```python
import functools
import math

import jax
import jax.numpy as jnp
from jax import lax
from jax.experimental import pallas as pl
from jax.experimental.pallas import tpu as pltpu
from jax.sharding import PartitionSpec as P

TB = 128
BLK = 256
PARTS = 4
ORDER = (2, 1, 3, 0)
LAGS = 4
VMEM_BYTES = 60 * 1024 * 1024
BF16 = jnp.bfloat16
F32 = jnp.float32


def dot(left, right, contract=((1,), (0,))):
    return lax.dot_general(left, right, (contract, ((), ())), preferred_element_type=F32)


def reversal(size):
    rows = lax.broadcasted_iota(jnp.int32, (size, size), 0)
    cols = lax.broadcasted_iota(jnp.int32, (size, size), 1)
    return (rows + cols == size - 1).astype(F32).astype(BF16)


def kernel(
    ns, nc, nu,
    q_hbm, k_hbm, v_hbm, w_hbm, og_hbm,
    rc, g2,
    q_v, k_v, v_v, w_v, og_v,
    xa, ra, sd, mb, rb, fs, f1, f1s, f2,
    tt, xf, xz0, xz8, gb, gjf, glt, lhs, acc, yst,
    lhe, xd, rd, mc, fgm, fgo, fgt, g1, g1s,
    in_sem, a_send, a_recv, b_send, b_recv, f_send, f_recv,
    d_send, d_recv, c_send, c_recv, g_send, g_recv, h_send, h_recv,
):
    me_s, me_c = lax.axis_index("seq"), lax.axis_index("ch")
    ny = ns // nu
    me_y, me_u = me_s // nu, lax.rem(me_s, nu)
    pr = ns // PARTS
    nb = ns * TB // BLK
    rows = nb * nc
    msg = 2 * nc
    norm = float((ns * TB) ** -0.5)
    lags = min(LAGS, nb)
    my_part = me_s // pr
    nq = nc // 2
    me_p, me_q = me_c // nq, lax.rem(me_c, nq)

    def copy_in(i, src, dst):
        return pltpu.make_async_copy(src, dst, in_sem.at[i])

    loads = [
        copy_in(0, k_hbm, k_v),
        copy_in(1, v_hbm, v_v),
        copy_in(2, og_hbm, og_v),
        copy_in(3, q_hbm, q_v),
        copy_in(4, w_hbm.at[pl.ds(pl.multiple_of(me_q * ns, ns), ns)], w_v.at[0]),
        copy_in(5, w_hbm.at[pl.ds(pl.multiple_of((me_q + nq) * ns, ns), ns)], w_v.at[1]),
    ]
    for load in loads:
        load.start()

    barrier = pltpu.get_barrier_semaphore()

    def greet_seq(o, carry):
        pl.semaphore_signal(barrier, inc=1, device_id={"seq": lax.rem(me_s + o, ns)})
        return carry

    def greet_ch(o, carry):
        pl.semaphore_signal(barrier, inc=1, device_id={"ch": lax.rem(me_c + o, nc)})
        return carry

    lax.fori_loop(1, nc, greet_ch, 0)
    lax.fori_loop(1, ns, greet_seq, 0)

    for load in loads:
        load.wait()

    for c in range(nc):
        f, q = c // nq, c % nq
        for m in range(PARTS):
            at = pl.ds(c * ns + m * pr, pr)
            xa[m, q, f] = (k_v[at].astype(F32) * v_v[at].astype(F32)).astype(BF16)
            xa[m, q, 2 + f] = (og_v[at].astype(F32) * q_v[at].astype(F32)).astype(BF16)
    for f in range(2):
        rows_f = w_v[f].astype(F32)
        for y in range(ny):
            fs[(2 * y + f) * nu : (2 * y + f + 1) * nu] = rows_f[y * nu : (y + 1) * nu]

    pl.semaphore_wait(barrier, ns - 1 + nc - 1)

    def tile(ref, i, size):
        return ref.at[pl.ds(pl.multiple_of(i * size, size), size)]

    def start_y(out_ref, in_ref, send_sem, recv_sem):
        size = out_ref.shape[0] // ny
        def push(o, carry):
            y = lax.rem(me_y + o, ny)
            pltpu.make_async_remote_copy(
                tile(out_ref, y, size), tile(in_ref, me_y, size), send_sem.at[0], recv_sem.at[0],
                device_id={"seq": y * nu + me_u},
            ).start()
            return carry

        lax.fori_loop(1, ny, push, 0)
        pltpu.make_async_copy(
            tile(out_ref, me_y, size), tile(in_ref, me_y, size), recv_sem.at[0]
        ).start()

    def turn_y_start_u(in_ref, mid_ref, end_ref, send_sem, recv_sem):
        wait_all(in_ref, recv_sem.at[0])
        size = in_ref.shape[0] // nu
        sets = size // ny
        for u in range(nu):
            for f in range(sets):
                at = u * size + f * ny
                mid_ref[at : at + ny] = in_ref[pl.ds(f * nu + u, ny, stride=sets * nu), :]

        def push(o, carry):
            u = lax.rem(me_u + o, nu)
            pltpu.make_async_remote_copy(
                tile(mid_ref, u, size), tile(end_ref, me_u, size), send_sem.at[1], recv_sem.at[1],
                device_id={"seq": me_y * nu + u},
            ).start()
            return carry

        lax.fori_loop(1, nu, push, 0)
        pltpu.make_async_copy(
            tile(mid_ref, me_u, size), tile(end_ref, me_u, size), recv_sem.at[1]
        ).start()

    def start_ch(out_ref, in_ref, send_sem, recv_sem):
        for kappa in ORDER:
            m = lax.rem(my_part + kappa, PARTS)

            def push(o, carry):
                q = lax.rem(me_q + o, nq)
                pltpu.make_async_remote_copy(
                    out_ref.at[m, q], in_ref.at[m, me_q], send_sem, recv_sem.at[kappa],
                    device_id={"ch": me_p * nq + q},
                ).start()
                return carry

            lax.fori_loop(1, nq, push, 0)
            pltpu.make_async_copy(out_ref.at[m, me_q], in_ref.at[m, me_q], recv_sem.at[kappa]).start()

    def turn_part(kappa, in_ref, mid_ref, recv_sem):
        m = lax.rem(my_part + kappa, PARTS)
        wait_all(in_ref.at[m], recv_sem.at[kappa])
        for q in range(nq):
            for kind in range(4):
                at = (kind * nq + q) * pr
                sd[at : at + pr] = in_ref[m, q, kind].astype(F32)
        for i in range(pr):
            mid_ref[kappa, i] = sd[pl.ds(i, msg, stride=pr), :].astype(BF16)

    def start_seq_part(kappa, mid_ref, end_ref, send_sem, recv_sem):
        m = lax.rem(my_part + kappa, PARTS)
        mine = lax.rem(me_s, pr)

        def push(o, carry):
            i = lax.rem(mine + o, pr)
            pltpu.make_async_remote_copy(
                mid_ref.at[kappa, i], end_ref.at[me_s], send_sem, recv_sem,
                device_id={"seq": m * pr + i},
            ).start()
            return carry

        lax.fori_loop(1 if kappa == 0 else 0, pr, push, 0)
        if kappa == 0:
            pltpu.make_async_copy(mid_ref.at[kappa, mine], end_ref.at[me_s], recv_sem).start()

    def wait_all(ref, sem):
        pltpu.make_async_copy(ref, ref, sem).wait()

    start_y(fs, f1, f_send, f_recv)
    start_ch(xa, ra, a_send, a_recv)
    turn_y_start_u(f1, f1s, f2, f_send, f_recv)
    for kappa in ORDER:
        turn_part(kappa, ra, mb, a_recv)
        start_seq_part(kappa, mb, rb, b_send, b_recv)

    sub = lax.broadcasted_iota(jnp.int32, (TB, TB), 0)
    lane = lax.broadcasted_iota(jnp.int32, (TB, TB), 1)
    keep = lane >= sub
    zero = jnp.zeros((TB, TB), F32)
    flip = reversal(BLK)
    wait_all(f2, f_recv.at[1])

    def skewed(tile):
        return pltpu.roll(tile, 0, 1, stride=1, stride_axis=0)

    def filter_row(f, s):
        at = (s % nu * 2 + f) * ny + s // nu
        return jnp.broadcast_to(f2[pl.ds(at, 1), :], (TB, TB))

    for f in range(2):
        tt[f, TB:BLK, 0:TB] = zero.astype(BF16)
        before = zero
        for d in range(nb):
            even, odd = skewed(filter_row(f, 2 * d)), skewed(filter_row(f, 2 * d + 1))
            block = jnp.where(keep, even, before).astype(BF16)
            tt[f, d * BLK : d * BLK + TB, 0:TB] = block
            tt[f, d * BLK + TB : (d + 1) * BLK, TB:BLK] = block
            block = jnp.where(keep, odd, even).astype(BF16)
            tt[f, d * BLK : d * BLK + TB, TB:BLK] = block
            tt[f, (d + 1) * BLK + TB : (d + 2) * BLK, 0:TB] = block
            before = odd

    lhs[:, 0 : lags * nc] = jnp.zeros((2, lags * nc, BLK), F32)
    xf[0:rows] = jnp.zeros((rows, BLK), F32)
    xf[2 * rows :] = jnp.zeros((nc, BLK), F32)

    wait_all(rb, b_recv)
    for j in range(nb):
        low, high = rb[2 * j].astype(F32), rb[2 * j + 1].astype(F32)
        xf[rows + j * nc : rows + (j + 1) * nc, 0:TB] = low[0:nc]
        xf[rows + j * nc : rows + (j + 1) * nc, TB:BLK] = high[0:nc]
        gjf[j * nc : (j + 1) * nc, 0:TB] = low[nc:msg]
        gjf[j * nc : (j + 1) * nc, TB:BLK] = high[nc:msg]
    gb[...] = gjf[...].astype(BF16)
    gjf[...] = dot(gb[...], flip)
    first_half = lax.broadcasted_iota(jnp.int32, (nc, BLK), 0) < nq

    def swap(rows_nc):
        return pltpu.roll(rows_nc, nq, 0)

    for j in range(nb):
        back = nb - 1 - j
        x_rows = xf[rows + j * nc : rows + (j + 1) * nc]
        g_rows = gjf[back * nc : (back + 1) * nc]
        at = pl.ds((lags + j) * nc, nc)
        lhs[0, at] = jnp.where(first_half, x_rows, swap(g_rows))
        lhs[1, at] = jnp.where(first_half, swap(x_rows), g_rows)
    for f in range(2):
        for e in range(lags):
            lhe[f, e] = lhs[f, pl.ds((lags - e) * nc, rows)].astype(BF16)

    for f in range(2):
        for first in range(0, nb, lags):
            count = (nb - first) * nc
            left = jnp.concatenate([lhe[f, e, 0:count] for e in range(lags)], axis=1)
            prod = dot(left, tt[f, first * BLK : (first + lags) * BLK])
            if first == 0:
                acc[f] = prod
            else:
                acc[f, first * nc :] += prod

    for j in range(nb):
        back = nb - 1 - j
        zeroth, other = acc[0, pl.ds(j * nc, nc)] * norm, acc[1, pl.ds(j * nc, nc)] * norm
        out = jnp.where(first_half, zeroth, swap(other))
        yst[2 * j * msg : 2 * j * msg + nc] = out[:, 0:TB]
        yst[(2 * j + 1) * msg : (2 * j + 1) * msg + nc] = out[:, TB:BLK]
        gjf[back * nc : (back + 1) * nc] = jnp.where(first_half, swap(zeroth), other)
    gjf[...] = dot(gjf[...].astype(BF16), flip)
    for j in range(nb):
        out = gjf[j * nc : (j + 1) * nc]
        yst[2 * j * msg + nc : (2 * j + 1) * msg] = out[:, 0:TB]
        yst[(2 * j + 1) * msg + nc : (2 * j + 2) * msg] = out[:, TB:BLK]

    for m in range(PARTS):
        for q in range(nq):
            for kind in range(4):
                begin = m * pr * msg + kind * nq + q
                xd[m, q, kind] = yst[pl.ds(begin, pr, stride=msg), :].astype(BF16)
    start_ch(xd, rd, d_send, d_recv)

    turned_g = dot(flip, gb[...], ((1,), (1,)))
    column = lax.rem(lax.broadcasted_iota(jnp.int32, (BLK, rows), 1), nc)
    glt[0:BLK] = jnp.where(column < nq, turned_g, 0.0).astype(BF16)
    glt[BLK:] = jnp.where(column < nq, 0.0, turned_g).astype(BF16)
    xz0[...] = xf[0 : 2 * rows].astype(BF16)
    xz8[...] = xf[nc : 2 * rows + nc].astype(BF16)
    over, before = [zero, zero], [zero, zero]
    for i in range(nb):
        low = (i // 2) * msg
        shifted = xz0[low + msg : low + msg + rows] if i % 2 else xz8[low : low + rows]
        both = dot(glt[...], shifted)
        for f in range(2):
            prod = both[f * BLK : (f + 1) * BLK]
            pair = (prod[0:TB, 0:TB] + over[f], prod[0:TB, TB:BLK] + prod[TB:BLK, 0:TB])
            for half, total in enumerate(pair):
                at = ns - 1 - (2 * i + half)
                turned = skewed(total)
                summed = jnp.sum(jnp.where(keep, turned, before[f]), axis=0, keepdims=True)
                fgm[f, at : at + 1] = summed
                before[f] = turned
            over[f] = prod[TB:BLK, TB:BLK]
    swapped = pltpu.make_async_remote_copy(
        fgm.at[1 - me_p], fgo, h_send, h_recv, device_id={"ch": (1 - me_p) * nq + me_q}
    )
    swapped.start()

    for kappa in ORDER:
        turn_part(kappa, rd, mc, d_recv)
        start_seq_part(kappa, mc, rc, c_send, c_recv)
    swapped.wait()
    fgt[...] = dot(((fgm[me_p] + fgo[...]) * norm).astype(BF16), reversal(TB))
    start_y(fgt, g1, g_send, g_recv)
    turn_y_start_u(g1, g1s, g2, g_send, g_recv)

    wait_all(rc, c_recv)
    wait_all(g2, g_recv.at[1])
    if nq > 1:
        wait_all(xa.at[:, pl.ds(0, nq - 1)], a_send)
        wait_all(xd.at[:, pl.ds(0, nq - 1)], d_send)
    for ref, sem in ((rb, b_send), (rc, c_send)):
        wait_all(ref.at[pl.ds(0, ns - 1)], sem)
    for ref, sem in ((f1, f_send), (g1, g_send)):
        size = ref.shape[0]
        wait_all(ref.at[pl.ds(0, size - size // ny)], sem.at[0])
        wait_all(ref.at[pl.ds(0, size - size // nu)], sem.at[1])


def finish(ns, nc, nu, rc, g2, k_v, v_v, og_v, qg_out, kg_out, vg_out, fg_out, rcf):
    msg, ny = 2 * nc, ns // nu
    rcf[...] = rc[...].astype(F32).reshape(ns * msg, TB)
    for c in range(nc):
        at = pl.ds(c * ns, ns)
        conv = rcf[pl.ds(c, ns, stride=msg), :]
        grad = rcf[pl.ds(nc + c, ns, stride=msg), :]
        qg_out[at] = (og_v[at].astype(F32) * conv).astype(BF16)
        kg_out[at] = (grad * v_v[at].astype(F32)).astype(BF16)
        vg_out[at] = (grad * k_v[at].astype(F32)).astype(BF16)
    for y in range(0, ny, 2):
        two = [g2[pl.ds(y + i, nu, stride=ny), :] for i in range(2)]
        fg_out[y * nu : (y + 2) * nu] = jnp.concatenate(two, axis=0).astype(BF16)


def shards(ns, nc, query_gate, key_gate, value_in, filter_weight, output_grad):
    local = query_gate.shape[0]
    nb, nu = ns * TB // BLK, math.isqrt(ns)
    ny = ns // nu
    rows, msg, pr = nb * nc, 2 * nc, ns // PARTS
    nq, lags = nc // 2, min(LAGS, nb)
    bf, f32 = (lambda *shape: pltpu.VMEM(shape, BF16)), (lambda *shape: pltpu.VMEM(shape, F32))
    one = pltpu.SemaphoreType.DMA(())
    two = pltpu.SemaphoreType.DMA((2,))
    some = pltpu.SemaphoreType.DMA((PARTS,))
    any_spec = pl.BlockSpec(memory_space=pl.ANY)
    vmem_spec = pl.BlockSpec(memory_space=pltpu.VMEM)
    moved, filter_part = pl.pallas_call(
        functools.partial(kernel, ns, nc, nu),
        out_shape=(
            jax.ShapeDtypeStruct((ns, msg, TB), BF16),
            jax.ShapeDtypeStruct((ns, TB), F32),
        ),
        in_specs=[any_spec] * 5,
        out_specs=(any_spec,) * 2,
        scratch_shapes=[
            bf(local, TB), bf(local, TB), bf(local, TB), bf(2, ns, TB), bf(local, TB),
            bf(PARTS, nq, 4, pr, TB), bf(PARTS, nq, 4, pr, TB), f32(msg * pr, TB),
            bf(PARTS, pr, msg, TB), bf(ns, msg, TB),
            f32(2 * ns, TB), f32(2 * ns, TB), f32(2 * ns, TB), f32(2 * ns, TB),
            bf(2, (nb + 1) * BLK, BLK), f32(2 * rows + nc, BLK), bf(2 * rows, BLK), bf(2 * rows, BLK),
            bf(rows, BLK), f32(rows, BLK), bf(2 * BLK, rows), f32(2, (lags + nb) * nc, BLK),
            f32(2, rows, BLK), f32(ns * msg, TB), bf(2, lags, rows, BLK),
            bf(PARTS, nq, 4, pr, TB), bf(PARTS, nq, 4, pr, TB),
            bf(PARTS, pr, msg, TB), f32(2, ns, TB), f32(ns, TB), f32(ns, TB), f32(ns, TB), f32(ns, TB),
            pltpu.SemaphoreType.DMA((6,)), one, some, one, one, two, two,
            one, some, one, one, two, two, one, one,
        ],
        compiler_params=pltpu.CompilerParams(
            collective_id=0, has_side_effects=True, vmem_limit_bytes=VMEM_BYTES
        ),
    )(query_gate, key_gate, value_in, filter_weight, output_grad)
    wide = jax.ShapeDtypeStruct((local, TB), BF16)
    return pl.pallas_call(
        functools.partial(finish, ns, nc, nu),
        out_shape=(wide, wide, wide, jax.ShapeDtypeStruct((ns, TB), BF16)),
        in_specs=[vmem_spec] * 5,
        out_specs=(vmem_spec,) * 4,
        scratch_shapes=[f32(ns * msg, TB)],
        compiler_params=pltpu.CompilerParams(vmem_limit_bytes=VMEM_BYTES),
    )(moved, filter_part, key_gate, value_in, output_grad)


def solution(mesh):
    ns, nc = mesh.shape["seq"], mesh.shape["ch"]
    placed = (P("ch", "seq"), P("ch", "seq"), P("ch", "seq"), P(None, "seq"), P("ch", "seq"))
    return jax.shard_map(
        functools.partial(shards, ns, nc),
        mesh=mesh,
        in_specs=placed,
        out_specs=(P("ch", "seq"),) * 4,
        check_vma=False,
    )
```

```python
import functools
import math

import jax
import jax.numpy as jnp
from jax import lax
from jax.experimental import pallas as pl
from jax.experimental.pallas import tpu as pltpu
from jax.sharding import PartitionSpec as P

TB = 128
BLK = 256
PARTS = 4
ORDER = (2, 1, 3, 0)
LAGS = 4
VMEM_BYTES = 60 * 1024 * 1024
BF16 = jnp.bfloat16
F32 = jnp.float32


def dot(left, right, contract=((1,), (0,))):
    return lax.dot_general(left, right, (contract, ((), ())), preferred_element_type=F32)


def reversal(size):
    rows = lax.broadcasted_iota(jnp.int32, (size, size), 0)
    cols = lax.broadcasted_iota(jnp.int32, (size, size), 1)
    return (rows + cols == size - 1).astype(F32).astype(BF16)


def kernel(
    ns, nc, nu,
    q_hbm, k_hbm, v_hbm, w_hbm, og_hbm,
    rc, g2,
    q_v, k_v, v_v, w_v, og_v,
    xa, ra, sd, mb, rb, fs, f1, f1s, f2,
    tt, xf, xz0, xz8, gb, gjf, glt, lhs, acc, yst,
    lhe, xd, rd, mc, fgm, fgt, g1, g1s,
    in_sem, a_send, a_recv, b_send, b_recv, f_send, f_recv,
    d_send, d_recv, c_send, c_recv, g_send, g_recv, h_send, h_recv, ready,
):
    me_s, me_c = lax.axis_index("seq"), lax.axis_index("ch")
    ny = ns // nu
    me_y, me_u = me_s // nu, lax.rem(me_s, nu)
    pr = ns // PARTS
    nb = ns * TB // BLK
    rows = nb * nc
    msg = 2 * nc
    norm = float((ns * TB) ** -0.5)
    lags = min(LAGS, nb)
    my_part = me_s // pr
    nq = nc // 2
    me_p, me_q = me_c // nq, lax.rem(me_c, nq)

    def copy_in(i, src, dst):
        return pltpu.make_async_copy(src, dst, in_sem.at[i])

    loads = [
        copy_in(0, k_hbm, k_v),
        copy_in(1, v_hbm, v_v),
        copy_in(2, og_hbm, og_v),
        copy_in(3, q_hbm, q_v),
        copy_in(4, w_hbm.at[pl.ds(pl.multiple_of(me_q * ns, ns), ns)], w_v.at[0]),
        copy_in(5, w_hbm.at[pl.ds(pl.multiple_of((me_q + nq) * ns, ns), ns)], w_v.at[1]),
    ]
    for load in loads:
        load.start()

    barrier = pltpu.get_barrier_semaphore()

    def greet_seq(o, carry):
        pl.semaphore_signal(barrier, inc=1, device_id={"seq": lax.rem(me_s + o, ns)})
        return carry

    def partner(y):
        return {"seq": y * nu + me_u, "ch": (1 - me_p) * nq + me_q}

    for o in range(1, nq):
        member = {"ch": me_p * nq + lax.rem(me_q + o, nq)}
        pl.semaphore_signal(barrier, inc=1, device_id=member)
    lax.fori_loop(1, ns, greet_seq, 0)

    @pl.when(me_p == 0)
    def _():
        for y in range(ny):
            pl.semaphore_signal(barrier, inc=1, device_id=partner(y))

    for load in loads:
        load.wait()

    for c in range(nc):
        f, q = c // nq, c % nq
        for m in range(PARTS):
            at = pl.ds(c * ns + m * pr, pr)
            xa[m, q, f] = (k_v[at].astype(F32) * v_v[at].astype(F32)).astype(BF16)
            xa[m, q, 2 + f] = (og_v[at].astype(F32) * q_v[at].astype(F32)).astype(BF16)
    for f in range(2):
        rows_f = w_v[f].astype(F32)
        for y in range(ny):
            fs[(2 * y + f) * nu : (2 * y + f + 1) * nu] = rows_f[y * nu : (y + 1) * nu]

    pl.semaphore_wait(barrier, ns - 1 + nq - 1 + me_p * ny)

    @pl.when(me_p == 1)
    def _():
        for y in range(ny):
            pl.semaphore_signal(ready, inc=1, device_id=partner(y))

    def tile(ref, i, size):
        return ref.at[pl.ds(pl.multiple_of(i * size, size), size)]

    def start_y(out_ref, in_ref, send_sem, recv_sem):
        size = out_ref.shape[0] // ny

        def push(o, carry):
            y = lax.rem(me_y + o, ny)
            pltpu.make_async_remote_copy(
                tile(out_ref, y, size), tile(in_ref, me_y, size), send_sem, recv_sem,
                device_id={"seq": y * nu + me_u},
            ).start()
            return carry

        lax.fori_loop(1, ny, push, 0)
        pltpu.make_async_copy(tile(out_ref, me_y, size), tile(in_ref, me_y, size), recv_sem).start()

    def turn_y_start_u(in_ref, mid_ref, end_ref, send_sem, recv_sem):
        size = in_ref.shape[0] // nu
        sets = size // ny
        for u in range(nu):
            for f in range(sets):
                at = u * size + f * ny
                mid_ref[at : at + ny] = in_ref[pl.ds(f * nu + u, ny, stride=sets * nu), :]

        def push(o, carry):
            u = lax.rem(me_u + o, nu)
            pltpu.make_async_remote_copy(
                tile(mid_ref, u, size), tile(end_ref, me_u, size), send_sem, recv_sem,
                device_id={"seq": me_y * nu + u},
            ).start()
            return carry

        lax.fori_loop(1, nu, push, 0)
        pltpu.make_async_copy(tile(mid_ref, me_u, size), tile(end_ref, me_u, size), recv_sem).start()

    def start_ch(out_ref, in_ref, send_sem, recv_sem):
        for kappa in ORDER:
            m = lax.rem(my_part + kappa, PARTS)

            def push(o, carry):
                q = lax.rem(me_q + o, nq)
                pltpu.make_async_remote_copy(
                    out_ref.at[m, q], in_ref.at[m, me_q], send_sem, recv_sem.at[kappa],
                    device_id={"ch": me_p * nq + q},
                ).start()
                return carry

            lax.fori_loop(1, nq, push, 0)
            pltpu.make_async_copy(out_ref.at[m, me_q], in_ref.at[m, me_q], recv_sem.at[kappa]).start()

    def turn_part(kappa, in_ref, mid_ref, recv_sem):
        m = lax.rem(my_part + kappa, PARTS)
        wait_all(in_ref.at[m], recv_sem.at[kappa])
        for q in range(nq):
            for kind in range(4):
                at = (kind * nq + q) * pr
                sd[at : at + pr] = in_ref[m, q, kind].astype(F32)
        for i in range(pr):
            mid_ref[kappa, i] = sd[pl.ds(i, msg, stride=pr), :].astype(BF16)

    def start_seq_part(kappa, mid_ref, end_ref, send_sem, recv_sem):
        m = lax.rem(my_part + kappa, PARTS)
        mine = lax.rem(me_s, pr)

        def push(o, carry):
            i = lax.rem(mine + o, pr)
            pltpu.make_async_remote_copy(
                mid_ref.at[kappa, i], end_ref.at[me_s], send_sem, recv_sem,
                device_id={"seq": m * pr + i},
            ).start()
            return carry

        lax.fori_loop(1 if kappa == 0 else 0, pr, push, 0)
        if kappa == 0:
            pltpu.make_async_copy(mid_ref.at[kappa, mine], end_ref.at[me_s], recv_sem).start()

    def wait_all(ref, sem):
        pltpu.make_async_copy(ref, ref, sem).wait()

    start_y(fs, f1, f_send.at[0], f_recv.at[0])
    start_ch(xa, ra, a_send, a_recv)
    wait_all(f1, f_recv.at[0])
    turn_y_start_u(f1, f1s, f2, f_send.at[1], f_recv.at[1])
    for kappa in ORDER:
        turn_part(kappa, ra, mb, a_recv)
        start_seq_part(kappa, mb, rb, b_send, b_recv)

    sub = lax.broadcasted_iota(jnp.int32, (TB, TB), 0)
    lane = lax.broadcasted_iota(jnp.int32, (TB, TB), 1)
    keep = lane >= sub
    zero = jnp.zeros((TB, TB), F32)
    flip = reversal(BLK)
    wait_all(f2, f_recv.at[1])

    def skewed(tile):
        return pltpu.roll(tile, 0, 1, stride=1, stride_axis=0)

    def filter_row(f, s):
        at = (s % nu * 2 + f) * ny + s // nu
        return jnp.broadcast_to(f2[pl.ds(at, 1), :], (TB, TB))

    for f in range(2):
        tt[f, TB:BLK, 0:TB] = zero.astype(BF16)
        before = zero
        for d in range(nb):
            even, odd = skewed(filter_row(f, 2 * d)), skewed(filter_row(f, 2 * d + 1))
            block = jnp.where(keep, even, before).astype(BF16)
            tt[f, d * BLK : d * BLK + TB, 0:TB] = block
            tt[f, d * BLK + TB : (d + 1) * BLK, TB:BLK] = block
            block = jnp.where(keep, odd, even).astype(BF16)
            tt[f, d * BLK : d * BLK + TB, TB:BLK] = block
            tt[f, (d + 1) * BLK + TB : (d + 2) * BLK, 0:TB] = block
            before = odd

    lhs[:, 0 : lags * nc] = jnp.zeros((2, lags * nc, BLK), F32)
    xf[0:rows] = jnp.zeros((rows, BLK), F32)
    xf[2 * rows :] = jnp.zeros((nc, BLK), F32)

    wait_all(rb, b_recv)
    for j in range(nb):
        low, high = rb[2 * j].astype(F32), rb[2 * j + 1].astype(F32)
        xf[rows + j * nc : rows + (j + 1) * nc, 0:TB] = low[0:nc]
        xf[rows + j * nc : rows + (j + 1) * nc, TB:BLK] = high[0:nc]
        gjf[j * nc : (j + 1) * nc, 0:TB] = low[nc:msg]
        gjf[j * nc : (j + 1) * nc, TB:BLK] = high[nc:msg]
    gb[...] = gjf[...].astype(BF16)
    gjf[...] = dot(gb[...], flip)
    first_half = lax.broadcasted_iota(jnp.int32, (nc, BLK), 0) < nq

    def swap(rows_nc):
        return pltpu.roll(rows_nc, nq, 0)

    turned_g = dot(flip, gb[...], ((1,), (1,)))
    column = lax.rem(lax.broadcasted_iota(jnp.int32, (BLK, rows), 1), nc)
    glt[0:BLK] = jnp.where(column < nq, turned_g, 0.0).astype(BF16)
    glt[BLK:] = jnp.where(column < nq, 0.0, turned_g).astype(BF16)
    xz0[...] = xf[0 : 2 * rows].astype(BF16)
    xz8[...] = xf[nc : 2 * rows + nc].astype(BF16)
    over, before = [zero, zero], [zero, zero]
    for i in range(nb):
        low = (i // 2) * msg
        shifted = xz0[low + msg : low + msg + rows] if i % 2 else xz8[low : low + rows]
        both = dot(glt[...], shifted)
        for f in range(2):
            prod = both[f * BLK : (f + 1) * BLK]
            pair = (prod[0:TB, 0:TB] + over[f], prod[0:TB, TB:BLK] + prod[TB:BLK, 0:TB])
            for half, total in enumerate(pair):
                at = ns - 1 - (2 * i + half)
                turned = skewed(total)
                summed = jnp.sum(jnp.where(keep, turned, before[f]), axis=0, keepdims=True)
                fgm[f, at : at + 1] = summed
                before[f] = turned
            over[f] = prod[TB:BLK, TB:BLK]
    start_y(fgm.at[me_p], g1.at[0], g_send.at[0], g_recv.at[0])

    @pl.when(me_p == 0)
    def _():
        pl.semaphore_wait(ready, ny)

    def push_other(o, carry):
        y = lax.rem(me_y + o, ny)
        pltpu.make_async_remote_copy(
            tile(fgm.at[1 - me_p], y, nu), tile(g1.at[1], me_y, nu), h_send, h_recv,
            device_id=partner(y),
        ).start()
        return carry

    lax.fori_loop(0, ny, push_other, 0)

    for j in range(nb):
        back = nb - 1 - j
        x_rows = xf[rows + j * nc : rows + (j + 1) * nc]
        g_rows = gjf[back * nc : (back + 1) * nc]
        at = pl.ds((lags + j) * nc, nc)
        lhs[0, at] = jnp.where(first_half, x_rows, swap(g_rows))
        lhs[1, at] = jnp.where(first_half, swap(x_rows), g_rows)
    for f in range(2):
        for e in range(lags):
            lhe[f, e] = lhs[f, pl.ds((lags - e) * nc, rows)].astype(BF16)

    for f in range(2):
        for first in range(0, nb, lags):
            count = (nb - first) * nc
            left = jnp.concatenate([lhe[f, e, 0:count] for e in range(lags)], axis=1)
            prod = dot(left, tt[f, first * BLK : (first + lags) * BLK])
            if first == 0:
                acc[f] = prod
            else:
                acc[f, first * nc :] += prod

    for j in range(nb):
        back = nb - 1 - j
        zeroth, other = acc[0, pl.ds(j * nc, nc)] * norm, acc[1, pl.ds(j * nc, nc)] * norm
        out = jnp.where(first_half, zeroth, swap(other))
        yst[2 * j * msg : 2 * j * msg + nc] = out[:, 0:TB]
        yst[(2 * j + 1) * msg : (2 * j + 1) * msg + nc] = out[:, TB:BLK]
        gjf[back * nc : (back + 1) * nc] = jnp.where(first_half, swap(zeroth), other)
    gjf[...] = dot(gjf[...].astype(BF16), flip)
    for j in range(nb):
        out = gjf[j * nc : (j + 1) * nc]
        yst[2 * j * msg + nc : (2 * j + 1) * msg] = out[:, 0:TB]
        yst[(2 * j + 1) * msg + nc : (2 * j + 2) * msg] = out[:, TB:BLK]

    for m in range(PARTS):
        for q in range(nq):
            for kind in range(4):
                begin = m * pr * msg + kind * nq + q
                xd[m, q, kind] = yst[pl.ds(begin, pr, stride=msg), :].astype(BF16)
    start_ch(xd, rd, d_send, d_recv)

    for step, kappa in enumerate(ORDER + (None,)):
        if step == 2:
            wait_all(g1.at[0], g_recv.at[0])
            wait_all(g1.at[1], h_recv)
            fgt[...] = dot(((g1[0] + g1[1]) * norm).astype(BF16), reversal(TB))
            turn_y_start_u(fgt, g1s, g2, g_send.at[1], g_recv.at[1])
        if kappa is not None:
            turn_part(kappa, rd, mc, d_recv)
            start_seq_part(kappa, mc, rc, c_send, c_recv)

    wait_all(rc, c_recv)
    wait_all(g2, g_recv.at[1])
    if nq > 1:
        wait_all(xa.at[:, pl.ds(0, nq - 1)], a_send)
        wait_all(xd.at[:, pl.ds(0, nq - 1)], d_send)
    for ref, sem in ((rb, b_send), (rc, c_send)):
        wait_all(ref.at[pl.ds(0, ns - 1)], sem)
    wait_all(g1.at[1], h_send)
    for ref, sem in ((f1, f_send), (g1s, g_send)):
        size = ref.shape[0]
        wait_all(ref.at[pl.ds(0, size - size // ny)], sem.at[0])
        wait_all(ref.at[pl.ds(0, size - size // nu)], sem.at[1])


def finish(ns, nc, nu, rc, g2, k_v, v_v, og_v, qg_out, kg_out, vg_out, fg_out, rcf):
    msg, ny = 2 * nc, ns // nu
    rcf[...] = rc[...].astype(F32).reshape(ns * msg, TB)
    for c in range(nc):
        at = pl.ds(c * ns, ns)
        conv = rcf[pl.ds(c, ns, stride=msg), :]
        grad = rcf[pl.ds(nc + c, ns, stride=msg), :]
        qg_out[at] = (og_v[at].astype(F32) * conv).astype(BF16)
        kg_out[at] = (grad * v_v[at].astype(F32)).astype(BF16)
        vg_out[at] = (grad * k_v[at].astype(F32)).astype(BF16)
    for y in range(0, ny, 2):
        two = [g2[pl.ds(y + i, nu, stride=ny), :] for i in range(2)]
        fg_out[y * nu : (y + 2) * nu] = jnp.concatenate(two, axis=0).astype(BF16)


def shards(ns, nc, query_gate, key_gate, value_in, filter_weight, output_grad):
    local = query_gate.shape[0]
    nb, nu = ns * TB // BLK, math.isqrt(ns)
    ny = ns // nu
    rows, msg, pr = nb * nc, 2 * nc, ns // PARTS
    nq, lags = nc // 2, min(LAGS, nb)
    bf, f32 = (lambda *shape: pltpu.VMEM(shape, BF16)), (lambda *shape: pltpu.VMEM(shape, F32))
    one = pltpu.SemaphoreType.DMA(())
    two = pltpu.SemaphoreType.DMA((2,))
    some = pltpu.SemaphoreType.DMA((PARTS,))
    any_spec = pl.BlockSpec(memory_space=pl.ANY)
    vmem_spec = pl.BlockSpec(memory_space=pltpu.VMEM)
    moved, filter_part = pl.pallas_call(
        functools.partial(kernel, ns, nc, nu),
        out_shape=(
            jax.ShapeDtypeStruct((ns, msg, TB), BF16),
            jax.ShapeDtypeStruct((ns, TB), F32),
        ),
        in_specs=[any_spec] * 5,
        out_specs=(any_spec,) * 2,
        scratch_shapes=[
            bf(local, TB), bf(local, TB), bf(local, TB), bf(2, ns, TB), bf(local, TB),
            bf(PARTS, nq, 4, pr, TB), bf(PARTS, nq, 4, pr, TB), f32(msg * pr, TB),
            bf(PARTS, pr, msg, TB), bf(ns, msg, TB),
            f32(2 * ns, TB), f32(2 * ns, TB), f32(2 * ns, TB), f32(2 * ns, TB),
            bf(2, (nb + 1) * BLK, BLK), f32(2 * rows + nc, BLK), bf(2 * rows, BLK), bf(2 * rows, BLK),
            bf(rows, BLK), f32(rows, BLK), bf(2 * BLK, rows), f32(2, (lags + nb) * nc, BLK),
            f32(2, rows, BLK), f32(ns * msg, TB), bf(2, lags, rows, BLK),
            bf(PARTS, nq, 4, pr, TB), bf(PARTS, nq, 4, pr, TB),
            bf(PARTS, pr, msg, TB), f32(2, ns, TB), f32(ns, TB), f32(2, ns, TB), f32(ns, TB),
            pltpu.SemaphoreType.DMA((6,)), one, some, one, one, two, two,
            one, some, one, one, two, two, one, one, pltpu.SemaphoreType.REGULAR,
        ],
        compiler_params=pltpu.CompilerParams(
            collective_id=0, has_side_effects=True, vmem_limit_bytes=VMEM_BYTES
        ),
    )(query_gate, key_gate, value_in, filter_weight, output_grad)
    wide = jax.ShapeDtypeStruct((local, TB), BF16)
    return pl.pallas_call(
        functools.partial(finish, ns, nc, nu),
        out_shape=(wide, wide, wide, jax.ShapeDtypeStruct((ns, TB), BF16)),
        in_specs=[vmem_spec] * 5,
        out_specs=(vmem_spec,) * 4,
        scratch_shapes=[f32(ns * msg, TB)],
        compiler_params=pltpu.CompilerParams(vmem_limit_bytes=VMEM_BYTES),
    )(moved, filter_part, key_gate, value_in, output_grad)


def solution(mesh):
    ns, nc = mesh.shape["seq"], mesh.shape["ch"]
    placed = (P("ch", "seq"), P("ch", "seq"), P("ch", "seq"), P(None, "seq"), P("ch", "seq"))
    return jax.shard_map(
        functools.partial(shards, ns, nc),
        mesh=mesh,
        in_specs=placed,
        out_specs=(P("ch", "seq"),) * 4,
        check_vma=False,
    )
```

```python
import functools
import math

import jax
import jax.numpy as jnp
from jax import lax
from jax.experimental import pallas as pl
from jax.experimental.pallas import tpu as pltpu
from jax.sharding import PartitionSpec as P

TB = 128
BLK = 256
PARTS = 4
ORDER = (2, 1, 3, 0)
LAGS = 4
VMEM_BYTES = 60 * 1024 * 1024
BF16 = jnp.bfloat16
F32 = jnp.float32


def dot(left, right, contract=((1,), (0,))):
    return lax.dot_general(left, right, (contract, ((), ())), preferred_element_type=F32)


def reversal(size):
    rows = lax.broadcasted_iota(jnp.int32, (size, size), 0)
    cols = lax.broadcasted_iota(jnp.int32, (size, size), 1)
    return (rows + cols == size - 1).astype(F32).astype(BF16)


def kernel(
    ns, nc, nu,
    q_hbm, k_hbm, v_hbm, w_hbm, og_hbm,
    rc, g2,
    q_v, k_v, v_v, w_v, og_v,
    xa, ra, sd, mb, rb, fs, f1, f1s, f2,
    tt, xf, xz0, xz8, gb, gjf, glt, lhs, acc, yst,
    lhe, xd, rd, mc, fgm, fgt, g1, g1s,
    in_sem, a_send, a_recv, b_send, b_recv, f_send, f_recv,
    d_send, d_recv, c_send, c_recv, g_send, g_recv, h_send, h_recv, ready,
):
    me_s, me_c = lax.axis_index("seq"), lax.axis_index("ch")
    ny = ns // nu
    me_y, me_u = me_s // nu, lax.rem(me_s, nu)
    pr = ns // PARTS
    nb = ns * TB // BLK
    rows = nb * nc
    msg = 2 * nc
    norm = float((ns * TB) ** -0.5)
    lags = min(LAGS, nb)
    my_part = me_s // pr
    nq = nc // 2
    me_p, me_q = me_c // nq, lax.rem(me_c, nq)

    def copy_in(i, src, dst):
        return pltpu.make_async_copy(src, dst, in_sem.at[i])

    loads = [
        copy_in(0, k_hbm, k_v),
        copy_in(1, v_hbm, v_v),
        copy_in(2, og_hbm, og_v),
        copy_in(3, q_hbm, q_v),
        copy_in(4, w_hbm.at[pl.ds(pl.multiple_of(me_q * ns, ns), ns)], w_v.at[0]),
        copy_in(5, w_hbm.at[pl.ds(pl.multiple_of((me_q + nq) * ns, ns), ns)], w_v.at[1]),
    ]
    for load in loads:
        load.start()

    barrier = pltpu.get_barrier_semaphore()

    def greet_seq(o, carry):
        pl.semaphore_signal(barrier, inc=1, device_id={"seq": lax.rem(me_s + o, ns)})
        return carry

    def partner(y):
        return {"seq": y * nu + me_u, "ch": (1 - me_p) * nq + me_q}

    for o in range(1, nq):
        member = {"ch": me_p * nq + lax.rem(me_q + o, nq)}
        pl.semaphore_signal(barrier, inc=1, device_id=member)
    for o in range(1, ns):
        greet_seq(o, 0)

    @pl.when(me_p == 0)
    def _():
        for y in range(ny):
            pl.semaphore_signal(barrier, inc=1, device_id=partner(y))

    for load in loads:
        load.wait()

    for c in range(nc):
        f, q = c // nq, c % nq
        for m in range(PARTS):
            at = pl.ds(c * ns + m * pr, pr)
            xa[m, q, f] = (k_v[at].astype(F32) * v_v[at].astype(F32)).astype(BF16)
            xa[m, q, 2 + f] = (og_v[at].astype(F32) * q_v[at].astype(F32)).astype(BF16)
    for f in range(2):
        rows_f = w_v[f].astype(F32)
        for y in range(ny):
            fs[(2 * y + f) * nu : (2 * y + f + 1) * nu] = rows_f[y * nu : (y + 1) * nu]

    pl.semaphore_wait(barrier, ns - 1 + nq - 1 + me_p * ny)

    @pl.when(me_p == 1)
    def _():
        for y in range(ny):
            pl.semaphore_signal(ready, inc=1, device_id=partner(y))

    def tile(ref, i, size):
        return ref.at[pl.ds(pl.multiple_of(i * size, size), size)]

    def start_y(out_ref, in_ref, send_sem, recv_sem):
        size = out_ref.shape[0] // ny

        def push(o, carry):
            y = lax.rem(me_y + o, ny)
            pltpu.make_async_remote_copy(
                tile(out_ref, y, size), tile(in_ref, me_y, size), send_sem, recv_sem,
                device_id={"seq": y * nu + me_u},
            ).start()
            return carry

        lax.fori_loop(1, ny, push, 0)
        pltpu.make_async_copy(tile(out_ref, me_y, size), tile(in_ref, me_y, size), recv_sem).start()

    def turn_y_start_u(in_ref, mid_ref, end_ref, send_sem, recv_sem):
        size = in_ref.shape[0] // nu
        sets = size // ny
        for u in range(nu):
            for f in range(sets):
                at = u * size + f * ny
                mid_ref[at : at + ny] = in_ref[pl.ds(f * nu + u, ny, stride=sets * nu), :]

        def push(o, carry):
            u = lax.rem(me_u + o, nu)
            pltpu.make_async_remote_copy(
                tile(mid_ref, u, size), tile(end_ref, me_u, size), send_sem, recv_sem,
                device_id={"seq": me_y * nu + u},
            ).start()
            return carry

        lax.fori_loop(1, nu, push, 0)
        pltpu.make_async_copy(tile(mid_ref, me_u, size), tile(end_ref, me_u, size), recv_sem).start()

    def start_ch(out_ref, in_ref, send_sem, recv_sem):
        for kappa in ORDER:
            m = lax.rem(my_part + kappa, PARTS)

            def push(o, carry):
                q = lax.rem(me_q + o, nq)
                pltpu.make_async_remote_copy(
                    out_ref.at[m, q], in_ref.at[m, me_q], send_sem, recv_sem.at[kappa],
                    device_id={"ch": me_p * nq + q},
                ).start()
                return carry

            lax.fori_loop(1, nq, push, 0)
            pltpu.make_async_copy(out_ref.at[m, me_q], in_ref.at[m, me_q], recv_sem.at[kappa]).start()

    def turn_part(kappa, in_ref, mid_ref, recv_sem):
        m = lax.rem(my_part + kappa, PARTS)
        wait_all(in_ref.at[m], recv_sem.at[kappa])
        for q in range(nq):
            for kind in range(4):
                at = (kind * nq + q) * pr
                sd[at : at + pr] = in_ref[m, q, kind].astype(F32)
        for i in range(pr):
            mid_ref[kappa, i] = sd[pl.ds(i, msg, stride=pr), :].astype(BF16)

    def start_seq_part(kappa, mid_ref, end_ref, send_sem, recv_sem):
        m = lax.rem(my_part + kappa, PARTS)
        mine = lax.rem(me_s, pr)

        def push(o, carry):
            i = lax.rem(mine + o, pr)
            pltpu.make_async_remote_copy(
                mid_ref.at[kappa, i], end_ref.at[me_s], send_sem, recv_sem,
                device_id={"seq": m * pr + i},
            ).start()
            return carry

        lax.fori_loop(1 if kappa == 0 else 0, pr, push, 0)
        if kappa == 0:
            pltpu.make_async_copy(mid_ref.at[kappa, mine], end_ref.at[me_s], recv_sem).start()

    def wait_all(ref, sem):
        pltpu.make_async_copy(ref, ref, sem).wait()

    start_ch(xa, ra, a_send, a_recv)
    start_y(fs, f1, f_send.at[0], f_recv.at[0])
    wait_all(f1, f_recv.at[0])
    turn_y_start_u(f1, f1s, f2, f_send.at[1], f_recv.at[1])
    for kappa in ORDER:
        turn_part(kappa, ra, mb, a_recv)
        start_seq_part(kappa, mb, rb, b_send, b_recv)

    sub = lax.broadcasted_iota(jnp.int32, (TB, TB), 0)
    lane = lax.broadcasted_iota(jnp.int32, (TB, TB), 1)
    keep = lane >= sub
    zero = jnp.zeros((TB, TB), F32)
    flip = reversal(BLK)
    wait_all(f2, f_recv.at[1])

    def skewed(tile):
        return pltpu.roll(tile, 0, 1, stride=1, stride_axis=0)

    def filter_row(f, s):
        at = (s % nu * 2 + f) * ny + s // nu
        return jnp.broadcast_to(f2[pl.ds(at, 1), :], (TB, TB))

    for f in range(2):
        tt[f, TB:BLK, 0:TB] = zero.astype(BF16)
        before = zero
        for d in range(nb):
            even, odd = skewed(filter_row(f, 2 * d)), skewed(filter_row(f, 2 * d + 1))
            block = jnp.where(keep, even, before).astype(BF16)
            tt[f, d * BLK : d * BLK + TB, 0:TB] = block
            tt[f, d * BLK + TB : (d + 1) * BLK, TB:BLK] = block
            block = jnp.where(keep, odd, even).astype(BF16)
            tt[f, d * BLK : d * BLK + TB, TB:BLK] = block
            tt[f, (d + 1) * BLK + TB : (d + 2) * BLK, 0:TB] = block
            before = odd

    lhs[:, 0 : lags * nc] = jnp.zeros((2, lags * nc, BLK), F32)
    xf[0:rows] = jnp.zeros((rows, BLK), F32)
    xf[2 * rows :] = jnp.zeros((nc, BLK), F32)

    wait_all(rb, b_recv)
    for j in range(nb):
        low, high = rb[2 * j].astype(F32), rb[2 * j + 1].astype(F32)
        xf[rows + j * nc : rows + (j + 1) * nc, 0:TB] = low[0:nc]
        xf[rows + j * nc : rows + (j + 1) * nc, TB:BLK] = high[0:nc]
        gjf[j * nc : (j + 1) * nc, 0:TB] = low[nc:msg]
        gjf[j * nc : (j + 1) * nc, TB:BLK] = high[nc:msg]
    gb[...] = gjf[...].astype(BF16)
    gjf[...] = dot(gb[...], flip)
    first_half = lax.broadcasted_iota(jnp.int32, (nc, BLK), 0) < nq

    def swap(rows_nc):
        return pltpu.roll(rows_nc, nq, 0)

    def filter_gradient():
        turned_g = dot(flip, gb[...], ((1,), (1,)))
        column = lax.rem(lax.broadcasted_iota(jnp.int32, (BLK, rows), 1), nc)
        glt[0:BLK] = jnp.where(column < nq, turned_g, 0.0).astype(BF16)
        glt[BLK:] = jnp.where(column < nq, 0.0, turned_g).astype(BF16)
        xz0[...] = xf[0 : 2 * rows].astype(BF16)
        xz8[...] = xf[nc : 2 * rows + nc].astype(BF16)
        over, before = [zero, zero], [zero, zero]
        for i in range(nb):
            low = (i // 2) * msg
            shifted = xz0[low + msg : low + msg + rows] if i % 2 else xz8[low : low + rows]
            both = dot(glt[...], shifted)
            for f in range(2):
                prod = both[f * BLK : (f + 1) * BLK]
                pair = (prod[0:TB, 0:TB] + over[f], prod[0:TB, TB:BLK] + prod[TB:BLK, 0:TB])
                for half, total in enumerate(pair):
                    at = ns - 1 - (2 * i + half)
                    turned = skewed(total)
                    summed = jnp.sum(jnp.where(keep, turned, before[f]), axis=0, keepdims=True)
                    fgm[f, at : at + 1] = summed
                    before[f] = turned
                over[f] = prod[TB:BLK, TB:BLK]
        start_y(fgm.at[me_p], g1.at[0], g_send.at[0], g_recv.at[0])

        @pl.when(me_p == 0)
        def _():
            pl.semaphore_wait(ready, ny)

        def push_other(o, carry):
            y = lax.rem(me_y + o, ny)
            pltpu.make_async_remote_copy(
                tile(fgm.at[1 - me_p], y, nu), tile(g1.at[1], me_y, nu), h_send, h_recv,
                device_id=partner(y),
            ).start()
            return carry

        lax.fori_loop(0, ny, push_other, 0)

    pl.when(me_p == 1)(filter_gradient)

    for j in range(nb):
        back = nb - 1 - j
        x_rows = xf[rows + j * nc : rows + (j + 1) * nc]
        g_rows = gjf[back * nc : (back + 1) * nc]
        at = pl.ds((lags + j) * nc, nc)
        lhs[0, at] = jnp.where(first_half, x_rows, swap(g_rows))
        lhs[1, at] = jnp.where(first_half, swap(x_rows), g_rows)
    for f in range(2):
        for e in range(lags):
            lhe[f, e] = lhs[f, pl.ds((lags - e) * nc, rows)].astype(BF16)

    for f in range(2):
        for first in range(0, nb, lags):
            count = (nb - first) * nc
            left = jnp.concatenate([lhe[f, e, 0:count] for e in range(lags)], axis=1)
            prod = dot(left, tt[f, first * BLK : (first + lags) * BLK])
            if first == 0:
                acc[f] = prod
            else:
                acc[f, first * nc :] += prod

    for j in range(nb):
        back = nb - 1 - j
        zeroth, other = acc[0, pl.ds(j * nc, nc)] * norm, acc[1, pl.ds(j * nc, nc)] * norm
        out = jnp.where(first_half, zeroth, swap(other))
        yst[2 * j * msg : 2 * j * msg + nc] = out[:, 0:TB]
        yst[(2 * j + 1) * msg : (2 * j + 1) * msg + nc] = out[:, TB:BLK]
        gjf[back * nc : (back + 1) * nc] = jnp.where(first_half, swap(zeroth), other)
    gjf[...] = dot(gjf[...].astype(BF16), flip)
    for j in range(nb):
        out = gjf[j * nc : (j + 1) * nc]
        yst[2 * j * msg + nc : (2 * j + 1) * msg] = out[:, 0:TB]
        yst[(2 * j + 1) * msg + nc : (2 * j + 2) * msg] = out[:, TB:BLK]

    for m in range(PARTS):
        for q in range(nq):
            for kind in range(4):
                begin = m * pr * msg + kind * nq + q
                xd[m, q, kind] = yst[pl.ds(begin, pr, stride=msg), :].astype(BF16)
    start_ch(xd, rd, d_send, d_recv)

    pl.when(me_p == 0)(filter_gradient)

    for step, kappa in enumerate(ORDER + (None,)):
        if step == 3:
            wait_all(g1.at[0], g_recv.at[0])
            wait_all(g1.at[1], h_recv)
            fgt[...] = dot(((g1[0] + g1[1]) * norm).astype(BF16), reversal(TB))
            turn_y_start_u(fgt, g1s, g2, g_send.at[1], g_recv.at[1])
        if kappa is not None:
            turn_part(kappa, rd, mc, d_recv)
            start_seq_part(kappa, mc, rc, c_send, c_recv)

    wait_all(rc, c_recv)
    wait_all(g2, g_recv.at[1])
    if nq > 1:
        wait_all(xa.at[:, pl.ds(0, nq - 1)], a_send)
        wait_all(xd.at[:, pl.ds(0, nq - 1)], d_send)
    for ref, sem in ((rb, b_send), (rc, c_send)):
        wait_all(ref.at[pl.ds(0, ns - 1)], sem)
    wait_all(g1.at[1], h_send)
    for ref, sem in ((f1, f_send), (g1s, g_send)):
        size = ref.shape[0]
        wait_all(ref.at[pl.ds(0, size - size // ny)], sem.at[0])
        wait_all(ref.at[pl.ds(0, size - size // nu)], sem.at[1])


def finish(ns, nc, nu, rc, g2, k_v, v_v, og_v, qg_out, kg_out, vg_out, fg_out, rcf):
    msg, ny = 2 * nc, ns // nu
    rcf[...] = rc[...].astype(F32).reshape(ns * msg, TB)
    for c in range(nc):
        at = pl.ds(c * ns, ns)
        conv = rcf[pl.ds(c, ns, stride=msg), :]
        grad = rcf[pl.ds(nc + c, ns, stride=msg), :]
        qg_out[at] = (og_v[at].astype(F32) * conv).astype(BF16)
        kg_out[at] = (grad * v_v[at].astype(F32)).astype(BF16)
        vg_out[at] = (grad * k_v[at].astype(F32)).astype(BF16)
    for y in range(0, ny, 2):
        two = [g2[pl.ds(y + i, nu, stride=ny), :] for i in range(2)]
        fg_out[y * nu : (y + 2) * nu] = jnp.concatenate(two, axis=0).astype(BF16)


def shards(ns, nc, query_gate, key_gate, value_in, filter_weight, output_grad):
    local = query_gate.shape[0]
    nb, nu = ns * TB // BLK, math.isqrt(ns)
    ny = ns // nu
    rows, msg, pr = nb * nc, 2 * nc, ns // PARTS
    nq, lags = nc // 2, min(LAGS, nb)
    bf, f32 = (lambda *shape: pltpu.VMEM(shape, BF16)), (lambda *shape: pltpu.VMEM(shape, F32))
    one = pltpu.SemaphoreType.DMA(())
    two = pltpu.SemaphoreType.DMA((2,))
    some = pltpu.SemaphoreType.DMA((PARTS,))
    any_spec = pl.BlockSpec(memory_space=pl.ANY)
    vmem_spec = pl.BlockSpec(memory_space=pltpu.VMEM)
    moved, filter_part = pl.pallas_call(
        functools.partial(kernel, ns, nc, nu),
        out_shape=(
            jax.ShapeDtypeStruct((ns, msg, TB), BF16),
            jax.ShapeDtypeStruct((ns, TB), F32),
        ),
        in_specs=[any_spec] * 5,
        out_specs=(any_spec,) * 2,
        scratch_shapes=[
            bf(local, TB), bf(local, TB), bf(local, TB), bf(2, ns, TB), bf(local, TB),
            bf(PARTS, nq, 4, pr, TB), bf(PARTS, nq, 4, pr, TB), f32(msg * pr, TB),
            bf(PARTS, pr, msg, TB), bf(ns, msg, TB),
            f32(2 * ns, TB), f32(2 * ns, TB), f32(2 * ns, TB), f32(2 * ns, TB),
            bf(2, (nb + 1) * BLK, BLK), f32(2 * rows + nc, BLK), bf(2 * rows, BLK), bf(2 * rows, BLK),
            bf(rows, BLK), f32(rows, BLK), bf(2 * BLK, rows), f32(2, (lags + nb) * nc, BLK),
            f32(2, rows, BLK), f32(ns * msg, TB), bf(2, lags, rows, BLK),
            bf(PARTS, nq, 4, pr, TB), bf(PARTS, nq, 4, pr, TB),
            bf(PARTS, pr, msg, TB), f32(2, ns, TB), f32(ns, TB), f32(2, ns, TB), f32(ns, TB),
            pltpu.SemaphoreType.DMA((6,)), one, some, one, one, two, two,
            one, some, one, one, two, two, one, one, pltpu.SemaphoreType.REGULAR,
        ],
        compiler_params=pltpu.CompilerParams(
            collective_id=0, has_side_effects=True, vmem_limit_bytes=VMEM_BYTES
        ),
    )(query_gate, key_gate, value_in, filter_weight, output_grad)
    wide = jax.ShapeDtypeStruct((local, TB), BF16)
    return pl.pallas_call(
        functools.partial(finish, ns, nc, nu),
        out_shape=(wide, wide, wide, jax.ShapeDtypeStruct((ns, TB), BF16)),
        in_specs=[vmem_spec] * 5,
        out_specs=(vmem_spec,) * 4,
        scratch_shapes=[f32(ns * msg, TB)],
        compiler_params=pltpu.CompilerParams(vmem_limit_bytes=VMEM_BYTES),
    )(moved, filter_part, key_gate, value_in, output_grad)


def solution(mesh):
    ns, nc = mesh.shape["seq"], mesh.shape["ch"]
    placed = (P("ch", "seq"), P("ch", "seq"), P("ch", "seq"), P(None, "seq"), P("ch", "seq"))
    return jax.shard_map(
        functools.partial(shards, ns, nc),
        mesh=mesh,
        in_specs=placed,
        out_specs=(P("ch", "seq"),) * 4,
        check_vma=False,
    )
```

```python
import functools
import math

import jax
import jax.numpy as jnp
from jax import lax
from jax.experimental import pallas as pl
from jax.experimental.pallas import tpu as pltpu
from jax.sharding import PartitionSpec as P

TB = 128
BLK = 256
PARTS = 4
ORDER = (2, 1, 3, 0)
LAGS = 4
VMEM_BYTES = 60 * 1024 * 1024
BF16 = jnp.bfloat16
F32 = jnp.float32


def dot(left, right, contract=((1,), (0,))):
    return lax.dot_general(left, right, (contract, ((), ())), preferred_element_type=F32)


def reversal(size):
    rows = lax.broadcasted_iota(jnp.int32, (size, size), 0)
    cols = lax.broadcasted_iota(jnp.int32, (size, size), 1)
    return (rows + cols == size - 1).astype(F32).astype(BF16)


def kernel(
    ns, nc, nu,
    q_hbm, k_hbm, v_hbm, w_hbm, og_hbm,
    rc, g2,
    q_v, k_v, v_v, w_v, og_v,
    xa, ra, sd, mb, rb, fs, f1, f1s, f2,
    tt, xf, xz0, xz8, gb, gjf, glt, lhs, acc, yst,
    lhe, xd, rd, mc, fgm, fgt, g1, g1s,
    in_sem, a_send, a_recv, b_send, b_recv, f_send, f_recv,
    d_send, d_recv, c_send, c_recv, g_send, g_recv, h_send, h_recv, ready,
):
    me_s, me_c = lax.axis_index("seq"), lax.axis_index("ch")
    ny = ns // nu
    me_y, me_u = me_s // nu, lax.rem(me_s, nu)
    pr = ns // PARTS
    nb = ns * TB // BLK
    rows = nb * nc
    msg = 2 * nc
    norm = float((ns * TB) ** -0.5)
    lags = min(LAGS, nb)
    my_part = me_s // pr
    nq = nc // 2
    me_p, me_q = me_c // nq, lax.rem(me_c, nq)

    def copy_in(i, src, dst):
        return pltpu.make_async_copy(src, dst, in_sem.at[i])

    loads = [
        copy_in(0, k_hbm, k_v),
        copy_in(1, v_hbm, v_v),
        copy_in(2, og_hbm, og_v),
        copy_in(3, q_hbm, q_v),
        copy_in(4, w_hbm.at[pl.ds(pl.multiple_of(me_q * ns, ns), ns)], w_v.at[0]),
        copy_in(5, w_hbm.at[pl.ds(pl.multiple_of((me_q + nq) * ns, ns), ns)], w_v.at[1]),
    ]
    for load in loads:
        load.start()

    barrier = pltpu.get_barrier_semaphore()

    def greet_seq(o, carry):
        pl.semaphore_signal(barrier, inc=1, device_id={"seq": lax.rem(me_s + o, ns)})
        return carry

    def partner(y):
        return {"seq": y * nu + me_u, "ch": (1 - me_p) * nq + me_q}

    for o in range(1, nq):
        member = {"ch": me_p * nq + lax.rem(me_q + o, nq)}
        pl.semaphore_signal(barrier, inc=1, device_id=member)
    for o in range(1, ns):
        greet_seq(o, 0)

    @pl.when(me_p == 0)
    def _():
        for y in range(ny):
            pl.semaphore_signal(barrier, inc=1, device_id=partner(y))

    for load in loads:
        load.wait()

    for c in range(nc):
        f, q = c // nq, c % nq
        for m in range(PARTS):
            at = pl.ds(c * ns + m * pr, pr)
            xa[m, q, f] = (k_v[at].astype(F32) * v_v[at].astype(F32)).astype(BF16)
            xa[m, q, 2 + f] = (og_v[at].astype(F32) * q_v[at].astype(F32)).astype(BF16)
    for f in range(2):
        rows_f = w_v[f].astype(F32)
        for y in range(ny):
            fs[(2 * y + f) * nu : (2 * y + f + 1) * nu] = rows_f[y * nu : (y + 1) * nu]

    pl.semaphore_wait(barrier, ns - 1 + nq - 1 + me_p * ny)

    @pl.when(me_p == 1)
    def _():
        for y in range(ny):
            pl.semaphore_signal(ready, inc=1, device_id=partner(y))

    def tile(ref, i, size):
        return ref.at[pl.ds(pl.multiple_of(i * size, size), size)]

    def start_y(out_ref, in_ref, send_sem, recv_sem):
        size = out_ref.shape[0] // ny

        def push(o, carry):
            y = lax.rem(me_y + o, ny)
            pltpu.make_async_remote_copy(
                tile(out_ref, y, size), tile(in_ref, me_y, size), send_sem, recv_sem,
                device_id={"seq": y * nu + me_u},
            ).start()
            return carry

        lax.fori_loop(1, ny, push, 0)
        pltpu.make_async_copy(tile(out_ref, me_y, size), tile(in_ref, me_y, size), recv_sem).start()

    def turn_y_start_u(in_ref, mid_ref, end_ref, send_sem, recv_sem):
        size = in_ref.shape[0] // nu
        sets = size // ny
        for u in range(nu):
            for f in range(sets):
                at = u * size + f * ny
                mid_ref[at : at + ny] = in_ref[pl.ds(f * nu + u, ny, stride=sets * nu), :]

        def push(o, carry):
            u = lax.rem(me_u + o, nu)
            pltpu.make_async_remote_copy(
                tile(mid_ref, u, size), tile(end_ref, me_u, size), send_sem, recv_sem,
                device_id={"seq": me_y * nu + u},
            ).start()
            return carry

        lax.fori_loop(1, nu, push, 0)
        pltpu.make_async_copy(tile(mid_ref, me_u, size), tile(end_ref, me_u, size), recv_sem).start()

    others = [lax.rem(me_q + o, nq) for o in range(1, nq)]
    if nq == 4:
        others = [nq - 1 - me_q, lax.rem(me_q + 2, nq), me_q + 1 - 2 * lax.rem(me_q, 2)]

    def start_ch(out_ref, in_ref, send_sem, recv_sem):
        for kappa in ORDER:
            m = lax.rem(my_part + kappa, PARTS)

            def push(q):
                pltpu.make_async_remote_copy(
                    out_ref.at[m, q], in_ref.at[m, me_q], send_sem, recv_sem.at[kappa],
                    device_id={"ch": me_p * nq + q},
                ).start()

            for q in others:
                push(q)
            pltpu.make_async_copy(out_ref.at[m, me_q], in_ref.at[m, me_q], recv_sem.at[kappa]).start()

    def turn_part(kappa, in_ref, mid_ref, recv_sem):
        m = lax.rem(my_part + kappa, PARTS)
        wait_all(in_ref.at[m], recv_sem.at[kappa])
        for q in range(nq):
            for kind in range(4):
                at = (kind * nq + q) * pr
                sd[at : at + pr] = in_ref[m, q, kind].astype(F32)
        for i in range(pr):
            mid_ref[kappa, i] = sd[pl.ds(i, msg, stride=pr), :].astype(BF16)

    def start_seq_part(kappa, mid_ref, end_ref, send_sem, recv_sem):
        m = lax.rem(my_part + kappa, PARTS)
        mine = lax.rem(me_s, pr)

        def push(o, carry):
            i = lax.rem(mine + o, pr)
            pltpu.make_async_remote_copy(
                mid_ref.at[kappa, i], end_ref.at[me_s], send_sem, recv_sem,
                device_id={"seq": m * pr + i},
            ).start()
            return carry

        for o in range(1 if kappa == 0 else 0, pr):
            push(o, 0)
        if kappa == 0:
            pltpu.make_async_copy(mid_ref.at[kappa, mine], end_ref.at[me_s], recv_sem).start()

    def wait_all(ref, sem):
        pltpu.make_async_copy(ref, ref, sem).wait()

    start_ch(xa, ra, a_send, a_recv)
    start_y(fs, f1, f_send.at[0], f_recv.at[0])
    wait_all(f1, f_recv.at[0])
    turn_y_start_u(f1, f1s, f2, f_send.at[1], f_recv.at[1])
    for kappa in ORDER:
        turn_part(kappa, ra, mb, a_recv)
        start_seq_part(kappa, mb, rb, b_send, b_recv)

    sub = lax.broadcasted_iota(jnp.int32, (TB, TB), 0)
    lane = lax.broadcasted_iota(jnp.int32, (TB, TB), 1)
    keep = lane >= sub
    zero = jnp.zeros((TB, TB), F32)
    flip = reversal(BLK)
    wait_all(f2, f_recv.at[1])

    def skewed(tile):
        return pltpu.roll(tile, 0, 1, stride=1, stride_axis=0)

    def filter_row(f, s):
        at = (s % nu * 2 + f) * ny + s // nu
        return jnp.broadcast_to(f2[pl.ds(at, 1), :], (TB, TB))

    for f in range(2):
        tt[f, TB:BLK, 0:TB] = zero.astype(BF16)
        before = zero
        for d in range(nb):
            even, odd = skewed(filter_row(f, 2 * d)), skewed(filter_row(f, 2 * d + 1))
            block = jnp.where(keep, even, before).astype(BF16)
            tt[f, d * BLK : d * BLK + TB, 0:TB] = block
            tt[f, d * BLK + TB : (d + 1) * BLK, TB:BLK] = block
            block = jnp.where(keep, odd, even).astype(BF16)
            tt[f, d * BLK : d * BLK + TB, TB:BLK] = block
            tt[f, (d + 1) * BLK + TB : (d + 2) * BLK, 0:TB] = block
            before = odd

    lhs[:, 0 : lags * nc] = jnp.zeros((2, lags * nc, BLK), F32)
    xf[0:rows] = jnp.zeros((rows, BLK), F32)
    xf[2 * rows :] = jnp.zeros((nc, BLK), F32)

    wait_all(rb, b_recv)
    for j in range(nb):
        low, high = rb[2 * j].astype(F32), rb[2 * j + 1].astype(F32)
        xf[rows + j * nc : rows + (j + 1) * nc, 0:TB] = low[0:nc]
        xf[rows + j * nc : rows + (j + 1) * nc, TB:BLK] = high[0:nc]
        gjf[j * nc : (j + 1) * nc, 0:TB] = low[nc:msg]
        gjf[j * nc : (j + 1) * nc, TB:BLK] = high[nc:msg]
    gb[...] = gjf[...].astype(BF16)
    gjf[...] = dot(gb[...], flip)
    first_half = lax.broadcasted_iota(jnp.int32, (nc, BLK), 0) < nq

    def swap(rows_nc):
        return pltpu.roll(rows_nc, nq, 0)

    def filter_gradient():
        turned_g = dot(flip, gb[...], ((1,), (1,)))
        column = lax.rem(lax.broadcasted_iota(jnp.int32, (BLK, rows), 1), nc)
        glt[0:BLK] = jnp.where(column < nq, turned_g, 0.0).astype(BF16)
        glt[BLK:] = jnp.where(column < nq, 0.0, turned_g).astype(BF16)
        xz0[...] = xf[0 : 2 * rows].astype(BF16)
        xz8[...] = xf[nc : 2 * rows + nc].astype(BF16)
        over, before = [zero, zero], [zero, zero]
        for i in range(nb):
            low = (i // 2) * msg
            shifted = xz0[low + msg : low + msg + rows] if i % 2 else xz8[low : low + rows]
            both = dot(glt[...], shifted)
            for f in range(2):
                prod = both[f * BLK : (f + 1) * BLK]
                pair = (prod[0:TB, 0:TB] + over[f], prod[0:TB, TB:BLK] + prod[TB:BLK, 0:TB])
                for half, total in enumerate(pair):
                    at = ns - 1 - (2 * i + half)
                    turned = skewed(total)
                    summed = jnp.sum(jnp.where(keep, turned, before[f]), axis=0, keepdims=True)
                    fgm[f, at : at + 1] = summed
                    before[f] = turned
                over[f] = prod[TB:BLK, TB:BLK]
        start_y(fgm.at[me_p], g1.at[0], g_send.at[0], g_recv.at[0])

        @pl.when(me_p == 0)
        def _():
            pl.semaphore_wait(ready, ny)

        def push_other(o, carry):
            y = lax.rem(me_y + o, ny)
            pltpu.make_async_remote_copy(
                tile(fgm.at[1 - me_p], y, nu), tile(g1.at[1], me_y, nu), h_send, h_recv,
                device_id=partner(y),
            ).start()
            return carry

        lax.fori_loop(0, ny, push_other, 0)

    pl.when(me_p == 1)(filter_gradient)

    for j in range(nb):
        back = nb - 1 - j
        x_rows = xf[rows + j * nc : rows + (j + 1) * nc]
        g_rows = gjf[back * nc : (back + 1) * nc]
        at = pl.ds((lags + j) * nc, nc)
        lhs[0, at] = jnp.where(first_half, x_rows, swap(g_rows))
        lhs[1, at] = jnp.where(first_half, swap(x_rows), g_rows)
    for f in range(2):
        for e in range(lags):
            lhe[f, e] = lhs[f, pl.ds((lags - e) * nc, rows)].astype(BF16)

    for f in range(2):
        for first in range(0, nb, lags):
            count = (nb - first) * nc
            left = jnp.concatenate([lhe[f, e, 0:count] for e in range(lags)], axis=1)
            prod = dot(left, tt[f, first * BLK : (first + lags) * BLK])
            if first == 0:
                acc[f] = prod
            else:
                acc[f, first * nc :] += prod

    for j in range(nb):
        back = nb - 1 - j
        zeroth, other = acc[0, pl.ds(j * nc, nc)] * norm, acc[1, pl.ds(j * nc, nc)] * norm
        out = jnp.where(first_half, zeroth, swap(other))
        yst[2 * j * msg : 2 * j * msg + nc] = out[:, 0:TB]
        yst[(2 * j + 1) * msg : (2 * j + 1) * msg + nc] = out[:, TB:BLK]
        gjf[back * nc : (back + 1) * nc] = jnp.where(first_half, swap(zeroth), other)
    gjf[...] = dot(gjf[...].astype(BF16), flip)
    for j in range(nb):
        out = gjf[j * nc : (j + 1) * nc]
        yst[2 * j * msg + nc : (2 * j + 1) * msg] = out[:, 0:TB]
        yst[(2 * j + 1) * msg + nc : (2 * j + 2) * msg] = out[:, TB:BLK]

    for m in range(PARTS):
        for q in range(nq):
            for kind in range(4):
                begin = m * pr * msg + kind * nq + q
                xd[m, q, kind] = yst[pl.ds(begin, pr, stride=msg), :].astype(BF16)
    start_ch(xd, rd, d_send, d_recv)

    pl.when(me_p == 0)(filter_gradient)

    for step, kappa in enumerate(ORDER + (None,)):
        if step == 3:
            wait_all(g1.at[0], g_recv.at[0])
            wait_all(g1.at[1], h_recv)
            fgt[...] = dot(((g1[0] + g1[1]) * norm).astype(BF16), reversal(TB))
            turn_y_start_u(fgt, g1s, g2, g_send.at[1], g_recv.at[1])
        if kappa is not None:
            turn_part(kappa, rd, mc, d_recv)
            start_seq_part(kappa, mc, rc, c_send, c_recv)

    wait_all(rc, c_recv)
    wait_all(g2, g_recv.at[1])
    if nq > 1:
        wait_all(xa.at[:, pl.ds(0, nq - 1)], a_send)
        wait_all(xd.at[:, pl.ds(0, nq - 1)], d_send)
    for ref, sem in ((rb, b_send), (rc, c_send)):
        wait_all(ref.at[pl.ds(0, ns - 1)], sem)
    wait_all(g1.at[1], h_send)
    for ref, sem in ((f1, f_send), (g1s, g_send)):
        size = ref.shape[0]
        wait_all(ref.at[pl.ds(0, size - size // ny)], sem.at[0])
        wait_all(ref.at[pl.ds(0, size - size // nu)], sem.at[1])


def finish(ns, nc, nu, rc, g2, k_v, v_v, og_v, qg_out, kg_out, vg_out, fg_out, rcf):
    msg, ny = 2 * nc, ns // nu
    rcf[...] = rc[...].astype(F32).reshape(ns * msg, TB)
    for c in range(nc):
        at = pl.ds(c * ns, ns)
        conv = rcf[pl.ds(c, ns, stride=msg), :]
        grad = rcf[pl.ds(nc + c, ns, stride=msg), :]
        qg_out[at] = (og_v[at].astype(F32) * conv).astype(BF16)
        kg_out[at] = (grad * v_v[at].astype(F32)).astype(BF16)
        vg_out[at] = (grad * k_v[at].astype(F32)).astype(BF16)
    for y in range(0, ny, 2):
        two = [g2[pl.ds(y + i, nu, stride=ny), :] for i in range(2)]
        fg_out[y * nu : (y + 2) * nu] = jnp.concatenate(two, axis=0).astype(BF16)


def shards(ns, nc, query_gate, key_gate, value_in, filter_weight, output_grad):
    local = query_gate.shape[0]
    nb, nu = ns * TB // BLK, math.isqrt(ns)
    ny = ns // nu
    rows, msg, pr = nb * nc, 2 * nc, ns // PARTS
    nq, lags = nc // 2, min(LAGS, nb)
    bf, f32 = (lambda *shape: pltpu.VMEM(shape, BF16)), (lambda *shape: pltpu.VMEM(shape, F32))
    one = pltpu.SemaphoreType.DMA(())
    two = pltpu.SemaphoreType.DMA((2,))
    some = pltpu.SemaphoreType.DMA((PARTS,))
    any_spec = pl.BlockSpec(memory_space=pl.ANY)
    vmem_spec = pl.BlockSpec(memory_space=pltpu.VMEM)
    moved, filter_part = pl.pallas_call(
        functools.partial(kernel, ns, nc, nu),
        out_shape=(
            jax.ShapeDtypeStruct((ns, msg, TB), BF16),
            jax.ShapeDtypeStruct((ns, TB), F32),
        ),
        in_specs=[any_spec] * 5,
        out_specs=(any_spec,) * 2,
        scratch_shapes=[
            bf(local, TB), bf(local, TB), bf(local, TB), bf(2, ns, TB), bf(local, TB),
            bf(PARTS, nq, 4, pr, TB), bf(PARTS, nq, 4, pr, TB), f32(msg * pr, TB),
            bf(PARTS, pr, msg, TB), bf(ns, msg, TB),
            f32(2 * ns, TB), f32(2 * ns, TB), f32(2 * ns, TB), f32(2 * ns, TB),
            bf(2, (nb + 1) * BLK, BLK), f32(2 * rows + nc, BLK), bf(2 * rows, BLK), bf(2 * rows, BLK),
            bf(rows, BLK), f32(rows, BLK), bf(2 * BLK, rows), f32(2, (lags + nb) * nc, BLK),
            f32(2, rows, BLK), f32(ns * msg, TB), bf(2, lags, rows, BLK),
            bf(PARTS, nq, 4, pr, TB), bf(PARTS, nq, 4, pr, TB),
            bf(PARTS, pr, msg, TB), f32(2, ns, TB), f32(ns, TB), f32(2, ns, TB), f32(ns, TB),
            pltpu.SemaphoreType.DMA((6,)), one, some, one, one, two, two,
            one, some, one, one, two, two, one, one, pltpu.SemaphoreType.REGULAR,
        ],
        compiler_params=pltpu.CompilerParams(
            collective_id=0, has_side_effects=True, vmem_limit_bytes=VMEM_BYTES
        ),
    )(query_gate, key_gate, value_in, filter_weight, output_grad)
    wide = jax.ShapeDtypeStruct((local, TB), BF16)
    return pl.pallas_call(
        functools.partial(finish, ns, nc, nu),
        out_shape=(wide, wide, wide, jax.ShapeDtypeStruct((ns, TB), BF16)),
        in_specs=[vmem_spec] * 5,
        out_specs=(vmem_spec,) * 4,
        scratch_shapes=[f32(ns * msg, TB)],
        compiler_params=pltpu.CompilerParams(vmem_limit_bytes=VMEM_BYTES),
    )(moved, filter_part, key_gate, value_in, output_grad)


def solution(mesh):
    ns, nc = mesh.shape["seq"], mesh.shape["ch"]
    placed = (P("ch", "seq"), P("ch", "seq"), P("ch", "seq"), P(None, "seq"), P("ch", "seq"))
    return jax.shard_map(
        functools.partial(shards, ns, nc),
        mesh=mesh,
        in_specs=placed,
        out_specs=(P("ch", "seq"),) * 4,
        check_vma=False,
    )
```
